256 devices in a mesh: region: 32 (over z, y), scan: 8 (over x, core).
Axes of the slice: x: 4, y: 4, z: 8, core: 2. Of those that a mesh axis runs over, the one named last changes fastest.
Arguments:
- object_field: float32 [2, 8192, 2048], P(None, 'region', 'scan'), may hold values from -5 to 5
- probe_modes: float32 [2, 8, 256, 256], replicated, may hold values from -4 to 4
- pattern: float32 [32, 8, 2, 256, 256], P('region', 'scan'), may hold values from 0.1 to 8
- rows_at: int32 [32, 8, 2], P('region', 'scan'), may hold values from 0 to 8191, as said below
- cols_at: int32 [32, 8, 2], P('region', 'scan'), may hold values from 0 to 2047, as said below
- object_step: float32 [1], replicated, may hold values from 0.1 to 0.4
- probe_step: float32 [1], replicated, may hold values from 0.05 to 0.1
Outputs:
- object_new: float32 [2, 8192, 2048], P(None, 'region', 'scan')
- probe_new: float32 [2, 8, 256, 256], replicated
The draws below stay inside these ranges and needn't reach their ends.
Inputs may be any that keep to these rules, and one draw needn't show every extreme that they name: `rows_at`: the windows of the 2 scans k of device (r, s) start at padded rows r * 256 + o + k * 128, with one o of that device and 0 <= o + k * 128 < 256. `cols_at`: the window of scan (r, s, k) starts at padded column s * 256 + o with 0 <= o < 256.
All inputs are finite; a program needn't handle non-finite values.
Results may differ from the reference program's by a relative error of at most 0.002.
The reference program's roundings to bfloat16 on the way count: a program that leaves them out, or rounds other values in their place, can miss the bound.
Values may be sent and summed in bfloat16 or wider, within the bound.
No kernel may reach another device: no remote copies, remote signals or barrier semaphores. Data moves between devices by JAX's collectives and lax.ppermute only.
A program may use at most 64 MiB of HBM per device.

```python
import math
import jax
import jax.numpy as jnp
from jax import lax

W = 256
MODES = 8
SCANS_DEV = 2
BLOCK_ROWS = 256
BLOCK_COLS = 256
ITERS = 1
OBJECT_ROWS = 8192
OBJECT_COLS = 2048
N_REGION = 32
N_SCAN = 8


def draw_rows_at(key, part):
    key = jax.random.fold_in(key, 11)
    spacing = W // 2
    room = BLOCK_ROWS - (SCANS_DEV - 1) * spacing
    offsets = jax.random.randint(key, (N_REGION, N_SCAN), 0, room)
    region_index = jnp.arange(N_REGION, dtype=jnp.int32)[:, None]
    scan_index = jnp.arange(N_SCAN, dtype=jnp.int32)[None, :]
    first_scan = (region_index == 0) & (scan_index == 0)
    last_scan = (region_index == N_REGION - 1) & (scan_index == N_SCAN - 1)
    offsets = jnp.where(first_scan, 0, jnp.where(last_scan, room - 1, offsets))
    lattice = jnp.arange(SCANS_DEV, dtype=jnp.int32)[None, None, :] * spacing
    return (region_index[:, :, None] * BLOCK_ROWS + offsets[:, :, None] + lattice).astype(jnp.int32)


def draw_cols_at(key, part):
    key = jax.random.fold_in(key, 23)
    offsets = jax.random.randint(key, (N_REGION, N_SCAN, SCANS_DEV), 0, BLOCK_COLS)
    region_index = jnp.arange(N_REGION, dtype=jnp.int32)[:, None, None]
    scan_index = jnp.arange(N_SCAN, dtype=jnp.int32)[None, :, None]
    slot_index = jnp.arange(SCANS_DEV, dtype=jnp.int32)[None, None, :]
    first_scan = (region_index == 0) & (scan_index == 0) & (slot_index == 0)
    last_scan = (region_index == N_REGION - 1) & (scan_index == N_SCAN - 1) & (slot_index == SCANS_DEV - 1)
    offsets = jnp.where(first_scan, 0, jnp.where(last_scan, BLOCK_COLS - 1, offsets))
    return (scan_index * BLOCK_COLS + offsets).astype(jnp.int32)


def level_of(own_key, dims, cuts, smallest, largest):
    loudness, own = 1.0, jax.random.fold_in(own_key, 6)
    for dim, shards_of in cuts:
        heights = jnp.exp(jax.random.uniform(jax.random.fold_in(own, dim), (shards_of,), jnp.float32, smallest / len(cuts), largest / len(cuts)))
        loudness = loudness * jnp.repeat(heights, dims[dim] // shards_of).reshape([-1 if axis == dim else 1 for axis in range(len(dims))])
    return loudness


def bell_draw(key, dims, scale, limit, split=(), kind=jnp.bfloat16):
    drawn = scale * jax.random.normal(key, dims, jnp.float32)
    if split:
        drawn = drawn * level_of(key, dims, split, -0.22, 0.18)
    return jnp.clip(drawn, -limit, limit).astype(kind)


def setup_inputs(seed: int = 0) -> dict:
    keys = jax.random.split(jax.random.key(seed), 8)
    return {
        "object_field": bell_draw(keys[0], (2, OBJECT_ROWS, OBJECT_COLS), 0.7, 5.0, ((1, 32), (2, 8)), jnp.float32),
        "probe_modes": bell_draw(keys[1], (2, MODES, W, W), 0.5, 4.0, (), jnp.float32),
        "pattern": jnp.clip(jnp.exp(math.log(8.0) - 4.3820266 * jax.random.uniform(keys[2], (N_REGION, N_SCAN, SCANS_DEV, W, W), jnp.float32) ** level_of(keys[2], (N_REGION, N_SCAN, SCANS_DEV, W, W), ((0, 32), (1, 8)), -0.2, 0.2)), 0.1, 8.0),
        "rows_at": draw_rows_at(jax.random.fold_in(keys[7], 71), 0),
        "cols_at": draw_cols_at(jax.random.fold_in(keys[7], 71), 0),
        "object_step": jnp.clip(jnp.exp(jax.random.uniform(keys[5], (ITERS,), jnp.float32, math.log(0.1), math.log(0.4))), 0.1, 0.4),
        "probe_step": jnp.clip(jnp.exp(jax.random.uniform(keys[6], (ITERS,), jnp.float32, math.log(0.05), math.log(0.1))), 0.05, 0.1),
    }


def fourier_tables(length):
    position = jnp.arange(length, dtype=jnp.int32)
    product = position[:, None] * position[None, :] % length
    angles = product.astype(jnp.float32) * (2.0 * math.pi / length)
    table_scale = 1.0 / math.sqrt(length)
    cosine_table = (jnp.cos(angles) * table_scale).astype(jnp.bfloat16)
    sine_table = (jnp.sin(angles) * table_scale).astype(jnp.bfloat16)
    return (cosine_table, sine_table)

def fourier_pass(real_part, imag_part, cosine_table, sine_table, direction):
    length = real_part.shape[-1]
    cosines_wide = cosine_table.astype(jnp.float32)
    sines_wide = sine_table.astype(jnp.float32)
    stacked = jnp.concatenate([real_part, imag_part], axis=2).astype(jnp.float32)
    first_cos = jnp.einsum('jk,mkn->mjn', cosines_wide, stacked)
    first_sin = jnp.einsum('jk,mkn->mjn', sines_wide, stacked)
    mid_real = (first_cos[:, :, :length] + direction * first_sin[:, :, length:]).astype(jnp.bfloat16)
    mid_imag = (first_cos[:, :, length:] - direction * first_sin[:, :, :length]).astype(jnp.bfloat16)
    row_stack = jnp.concatenate([mid_real, mid_imag], axis=1).astype(jnp.float32)
    second_cos = jnp.einsum('mjk,kn->mjn', row_stack, cosines_wide)
    second_sin = jnp.einsum('mjk,kn->mjn', row_stack, sines_wide)
    out_real = second_cos[:, :length] + direction * second_sin[:, length:]
    out_imag = second_cos[:, length:] - direction * second_sin[:, :length]
    return (out_real, out_imag)

def scan_gradients(window, probe_modes, pattern_block, cosine_table, sine_table):
    win_real = window[0].astype(jnp.float32)
    win_imag = window[1].astype(jnp.float32)
    probe_real = probe_modes[0]
    probe_imag = probe_modes[1]
    wave_real = (probe_real * win_real - probe_imag * win_imag).astype(jnp.bfloat16)
    wave_imag = (probe_real * win_imag + probe_imag * win_real).astype(jnp.bfloat16)
    far_real, far_imag = fourier_pass(wave_real, wave_imag, cosine_table, sine_table, 1.0)
    intensity = lax.optimization_barrier(jnp.sum(far_real * far_real + far_imag * far_imag, axis=0))
    amplitude = jnp.maximum(jnp.sqrt(intensity), 1.0)
    factor = 1.0 - jnp.sqrt(pattern_block) / amplitude
    back_real, back_imag = fourier_pass((factor * far_real).astype(jnp.bfloat16), (factor * far_imag).astype(jnp.bfloat16), cosine_table, sine_table, -1.0)
    object_real = lax.optimization_barrier(jnp.sum(probe_real * back_real + probe_imag * back_imag, axis=0))
    object_imag = lax.optimization_barrier(jnp.sum(probe_real * back_imag - probe_imag * back_real, axis=0))
    probe_grad_real = win_real * back_real + win_imag * back_imag
    probe_grad_imag = win_real * back_imag - win_imag * back_real
    return (jnp.stack([object_real, object_imag]), jnp.stack([probe_grad_real, probe_grad_imag]))

def reference(object_field, probe_modes, pattern, rows_at, cols_at, object_step, probe_step):
    cosine_table, sine_table = fourier_tables(W)
    half_width = W // 2
    scan_count = N_REGION * N_SCAN * SCANS_DEV
    pattern_flat = pattern.reshape(scan_count, W, W)
    rows_flat = rows_at.reshape(scan_count).astype(jnp.int32)
    cols_flat = cols_at.reshape(scan_count).astype(jnp.int32)
    anchor = jnp.zeros((), jnp.int32)
    for step_index in range(ITERS):
        padded = jnp.pad(object_field.astype(jnp.bfloat16), ((0, 0), (half_width, half_width), (half_width, half_width)))
        current_probe = probe_modes

        def visit_scan(running, inputs):
            grad_field, probe_total = running
            pattern_block, row_start, col_start = inputs
            window = lax.dynamic_slice(padded, (anchor, row_start, col_start), (2, W, W))
            object_term, probe_term = scan_gradients(window, current_probe, pattern_block, cosine_table, sine_table)
            current = lax.dynamic_slice(grad_field, (anchor, row_start, col_start), (2, W, W))
            grad_field = lax.dynamic_update_slice(grad_field, current + object_term, (anchor, row_start, col_start))
            return ((grad_field, probe_total + probe_term), None)
        initial = (jnp.zeros((2, OBJECT_ROWS + W, OBJECT_COLS + W), jnp.float32), jnp.zeros(probe_modes.shape, jnp.float32))
        (grad_field, probe_total), _ = lax.scan(visit_scan, initial, (pattern_flat, rows_flat, cols_flat))
        object_grad = grad_field[:, half_width:half_width + OBJECT_ROWS, half_width:half_width + OBJECT_COLS]
        object_field = object_field - object_step[step_index] * object_grad
        probe_modes = probe_modes - probe_step[step_index] * probe_total
    return (object_field, probe_modes)
```

```python
import math

import jax
import jax.numpy as jnp
from jax import lax
from jax.sharding import PartitionSpec as P


def padded_2(cells, sides, width):
    for axis, dim in sides:
        count = lax.axis_size(axis)
        ends = count - 1
        head = lax.slice_in_dim(cells, 0, width, axis=dim)
        tail = lax.slice_in_dim(cells, cells.shape[dim] - width, cells.shape[dim], axis=dim)
        cells = jnp.concatenate(
            [
                lax.ppermute(tail, axis, [(i, (i + 1) % count) for i in range(ends)]),
                cells,
                lax.ppermute(head, axis, [((i + 1) % count, i) for i in range(ends)]),
            ],
            axis=dim,
        )
    return cells


def fourier_tables(length):
    position = jnp.arange(length, dtype=jnp.int32)
    product = position[:, None] * position[None, :] % length
    angles = product.astype(jnp.float32) * (2.0 * math.pi / length)
    table_scale = 1.0 / math.sqrt(length)
    cosine_table = (jnp.cos(angles) * table_scale).astype(jnp.bfloat16)
    sine_table = (jnp.sin(angles) * table_scale).astype(jnp.bfloat16)
    return (cosine_table, sine_table)


def fourier_pass(real_part, imag_part, cosine_table, sine_table, direction):
    length = real_part.shape[-1]
    stacked = jnp.concatenate([real_part, imag_part], axis=2)
    first_cos = jnp.einsum("jk,mkn->mjn", cosine_table, stacked, preferred_element_type=jnp.float32)
    first_sin = jnp.einsum("jk,mkn->mjn", sine_table, stacked, preferred_element_type=jnp.float32)
    mid_real = (first_cos[:, :, :length] + direction * first_sin[:, :, length:]).astype(
        jnp.bfloat16
    )
    mid_imag = (first_cos[:, :, length:] - direction * first_sin[:, :, :length]).astype(
        jnp.bfloat16
    )
    row_stack = jnp.concatenate([mid_real, mid_imag], axis=1)
    second_cos = jnp.einsum(
        "mjk,kn->mjn", row_stack, cosine_table, preferred_element_type=jnp.float32
    )
    second_sin = jnp.einsum(
        "mjk,kn->mjn", row_stack, sine_table, preferred_element_type=jnp.float32
    )
    out_real = second_cos[:, :length] + direction * second_sin[:, length:]
    out_imag = second_cos[:, length:] - direction * second_sin[:, :length]
    return (out_real, out_imag)


def scan_gradients(window, probe_modes, pattern_block, cosine_table, sine_table):
    win_real = window[0].astype(jnp.float32)
    win_imag = window[1].astype(jnp.float32)
    probe_real = probe_modes[0]
    probe_imag = probe_modes[1]
    wave_real = (probe_real * win_real - probe_imag * win_imag).astype(jnp.bfloat16)
    wave_imag = (probe_real * win_imag + probe_imag * win_real).astype(jnp.bfloat16)
    far_real, far_imag = fourier_pass(wave_real, wave_imag, cosine_table, sine_table, 1.0)
    intensity = jnp.sum(far_real * far_real + far_imag * far_imag, axis=0)
    amplitude = jnp.maximum(jnp.sqrt(intensity), 1.0)
    factor = 1.0 - jnp.sqrt(pattern_block) / amplitude
    back_real, back_imag = fourier_pass(
        (factor * far_real).astype(jnp.bfloat16),
        (factor * far_imag).astype(jnp.bfloat16),
        cosine_table,
        sine_table,
        -1.0,
    )
    object_real = jnp.sum(probe_real * back_real + probe_imag * back_imag, axis=0)
    object_imag = jnp.sum(probe_real * back_imag - probe_imag * back_real, axis=0)
    probe_grad_real = win_real * back_real + win_imag * back_imag
    probe_grad_imag = win_real * back_imag - win_imag * back_real
    return (jnp.stack([object_real, object_imag]), jnp.stack([probe_grad_real, probe_grad_imag]))


def return_rims(grad_field, half_width):
    cols_rim = jnp.concatenate(
        [grad_field[:, :, :half_width], grad_field[:, :, -half_width:]], axis=2
    )
    cols_ext = padded_2(cols_rim, (("scan", 2),), half_width)
    core_block = grad_field[:, :, half_width:-half_width]
    core_block = core_block.at[:, :, :half_width].add(cols_ext[:, :, :half_width])
    core_block = core_block.at[:, :, -half_width:].add(cols_ext[:, :, -half_width:])
    rows_rim = jnp.concatenate([core_block[:, :half_width], core_block[:, -half_width:]], axis=1)
    rows_ext = padded_2(rows_rim, (("region", 1),), half_width)
    inner_block = core_block[:, half_width:-half_width]
    inner_block = inner_block.at[:, :half_width].add(rows_ext[:, :half_width])
    inner_block = inner_block.at[:, -half_width:].add(rows_ext[:, -half_width:])
    return inner_block


def axis_groups(kept):
    rows, cols = lax.axis_size("region"), lax.axis_size("scan")
    sizes = {"z": rows // 4, "y": 4, "x": cols // 2, "core": 2}
    groups = {}
    for device in range(rows * cols):
        place, rest = {}, device
        for name in ("core", "x", "y", "z"):
            place[name] = rest % sizes[name]
            rest = rest // sizes[name]
        key = tuple(place[name] for name in place if name not in kept)
        groups.setdefault(key, []).append(device)
    return [groups[key] for key in sorted(groups)]


def narrow(values, scale):
    return (values * (1.0 / scale)).astype(jnp.float16)


def widen(values, scale):
    return values.astype(jnp.float32) * scale


def exchange(parts, kept):
    return lax.all_to_all(parts, ("region", "scan"), 0, 0, axis_index_groups=axis_groups(kept))


def swap_cores(values):
    count = lax.axis_size("region") * lax.axis_size("scan")
    return lax.ppermute(values, ("region", "scan"), [(i, i ^ 1) for i in range(count)])


def sum_everywhere(term):
    _, modes, rows, cols = term.shape
    core = lax.axis_index("scan") % 2
    mine = lax.dynamic_index_in_dim(term, core, 0, keepdims=False)
    other = lax.dynamic_index_in_dim(term, 1 - core, 0, keepdims=False)
    pair = mine + widen(swap_cores(narrow(other, 8.0)), 8.0)
    plane = 16
    slab = modes * rows // plane
    pieces = exchange(narrow(pair, 16.0).reshape(plane, slab, cols), ("y", "x"))
    slab_sum = jnp.sum(widen(pieces, 16.0), axis=0)
    depth = lax.axis_size("region") // 4
    pieces = exchange(slab_sum.reshape(depth, slab // depth, cols), ("z",))
    total = narrow(jnp.sum(pieces, axis=0), 2048.0)
    total = exchange(jnp.broadcast_to(total, (depth, slab // depth, cols)), ("z",))
    total = exchange(jnp.broadcast_to(total.reshape(slab, cols), (plane, slab, cols)), ("y", "x"))
    total = total.reshape(modes, rows, cols)
    swapped = swap_cores(total)
    first = core == 0
    return widen(
        jnp.stack([jnp.where(first, total, swapped), jnp.where(first, swapped, total)]), 2048.0
    )


def on_device(object_field, probe_modes, pattern, rows_at, cols_at, object_step, probe_step):
    length = probe_modes.shape[-1]
    half_width = length // 2
    block_rows = object_field.shape[1]
    block_cols = object_field.shape[2]
    scan_slots = pattern.shape[2]
    cosine_table, sine_table = fourier_tables(length)
    row_offsets = rows_at[0, 0] % block_rows
    col_offsets = cols_at[0, 0] % block_cols
    anchor = jnp.zeros((), jnp.int32)
    padded = padded_2(object_field.astype(jnp.bfloat16), (("region", 1), ("scan", 2)), half_width)
    grad_field = jnp.zeros((2, block_rows + length, block_cols + length), jnp.float32)
    probe_term = jnp.zeros(probe_modes.shape, jnp.float32)
    for slot in range(scan_slots):
        row_offset = row_offsets[slot]
        col_offset = col_offsets[slot]
        window = lax.dynamic_slice(padded, (anchor, row_offset, col_offset), (2, length, length))
        object_term, slot_probe = scan_gradients(
            window, probe_modes, pattern[0, 0, slot], cosine_table, sine_table
        )
        current = lax.dynamic_slice(
            grad_field, (anchor, row_offset, col_offset), (2, length, length)
        )
        grad_field = lax.dynamic_update_slice(
            grad_field, current + object_term, (anchor, row_offset, col_offset)
        )
        probe_term = probe_term + slot_probe
    grad_block = return_rims(grad_field, half_width)
    object_field = object_field - object_step[0] * grad_block
    probe_total = sum_everywhere(probe_term)
    probe_modes = probe_modes - probe_step[0] * probe_total
    return (object_field, probe_modes)


def solution(mesh):
    return jax.shard_map(
        on_device,
        mesh=mesh,
        in_specs=(
            P(None, "region", "scan"),
            P(),
            P("region", "scan", None, None, None),
            P("region", "scan", None),
            P("region", "scan", None),
            P(),
            P(),
        ),
        out_specs=(P(None, "region", "scan"), P()),
        check_vma=False,
    )
```

```python
import math

import jax
import jax.numpy as jnp
import ml_dtypes
import numpy as np
from jax import lax
from jax.experimental import pallas as pl
from jax.experimental.pallas import tpu as pltpu
from jax.sharding import PartitionSpec as P


UNROLL = 4


def padded_2(cells, sides, width):
    for axis, dim in sides:
        count = lax.axis_size(axis)
        ends = count - 1
        head = lax.slice_in_dim(cells, 0, width, axis=dim)
        tail = lax.slice_in_dim(cells, cells.shape[dim] - width, cells.shape[dim], axis=dim)
        cells = jnp.concatenate(
            [
                lax.ppermute(tail, axis, [(i, (i + 1) % count) for i in range(ends)]),
                cells,
                lax.ppermute(head, axis, [((i + 1) % count, i) for i in range(ends)]),
            ],
            axis=dim,
        )
    return cells


def fourier_blocks(length):
    position = np.arange(length)
    angles = (position[:, None] * position[None, :] % length) * (2.0 * math.pi / length)
    table_scale = 1.0 / math.sqrt(length)
    cosine_table = (np.cos(angles) * table_scale).astype(ml_dtypes.bfloat16)
    sine_table = (np.sin(angles) * table_scale).astype(ml_dtypes.bfloat16)
    forward = np.block([[cosine_table, sine_table], [-sine_table, cosine_table]])
    return (jnp.asarray(forward), jnp.asarray(np.ascontiguousarray(forward.T)))


def fourier_pass(real_part, imag_part, left, right):
    length = real_part.shape[-1]
    stacked = jnp.concatenate([real_part, imag_part], axis=0)
    middle = jnp.dot(left, stacked, preferred_element_type=jnp.float32).astype(jnp.bfloat16)
    middle = jnp.concatenate([middle[:length], middle[length:]], axis=1)
    return jnp.dot(middle, right, preferred_element_type=jnp.float32)


def gradients_kernel(
    place_ref,
    block_ref,
    above_ref,
    below_ref,
    left_ref,
    right_ref,
    probe_ref,
    pattern_ref,
    forward_ref,
    backward_ref,
    grad_ref,
    mine_ref,
    other_ref,
    padded_ref,
    window_ref,
    far_ref,
    level_ref,
    object_ref,
    term_ref,
):
    modes, length = probe_ref.shape[1], probe_ref.shape[2]
    half = length // 2
    rows, cols = block_ref.shape[1], block_ref.shape[2]
    wide = padded_ref.shape[2]
    slots = pattern_ref.shape[0]
    padded_ref[:, half : half + rows, half : half + cols] = (
        block_ref[...].astype(jnp.bfloat16).astype(jnp.float32)
    )
    padded_ref[:, :half, half : half + cols] = above_ref[...].astype(jnp.float32)
    padded_ref[:, half + rows :, half : half + cols] = below_ref[...].astype(jnp.float32)
    padded_ref[:, :, :half] = left_ref[...].astype(jnp.float32)
    padded_ref[:, :, half + cols :] = right_ref[...].astype(jnp.float32)
    grad_ref[...] = jnp.zeros_like(grad_ref)
    first = place_ref[2, 0] == 0
    for slot in range(slots):
        row = place_ref[0, slot]
        col = place_ref[1, slot]
        shift = row % 8
        span = pl.ds(pl.multiple_of(row - shift, 8), length + 8)
        for part in range(2):
            strip = pltpu.roll(padded_ref[part, span, :], wide - col, 1)[:, :length]
            window_ref[part] = pltpu.roll(strip, length + 8 - shift, 0)[:length]

        level_ref[...] = jnp.zeros_like(level_ref)

        def go_forward(mode, carry):
            win_real, win_imag = window_ref[0], window_ref[1]
            probe_real, probe_imag = probe_ref[0, mode], probe_ref[1, mode]
            far = fourier_pass(
                (probe_real * win_real - probe_imag * win_imag).astype(jnp.bfloat16),
                (probe_real * win_imag + probe_imag * win_real).astype(jnp.bfloat16),
                forward_ref[...],
                backward_ref[...],
            )
            far_ref[mode] = far
            far_real, far_imag = far[:, :length], far[:, length:]
            level_ref[...] += far_real * far_real + far_imag * far_imag
            return carry

        lax.fori_loop(0, modes, go_forward, 0, unroll=UNROLL)
        amplitude = jnp.maximum(jnp.sqrt(level_ref[...]), 1.0)
        level_ref[...] = 1.0 - jnp.sqrt(pattern_ref[slot]) / amplitude
        object_ref[...] = jnp.zeros_like(object_ref)

        def go_back(mode, carry):
            factor = level_ref[...]
            far = far_ref[mode]
            back = fourier_pass(
                (factor * far[:, :length]).astype(jnp.bfloat16),
                (factor * far[:, length:]).astype(jnp.bfloat16),
                backward_ref[...],
                forward_ref[...],
            )
            back_real, back_imag = back[:, :length], back[:, length:]
            probe_real, probe_imag = probe_ref[0, mode], probe_ref[1, mode]
            object_ref[0] += probe_real * back_real + probe_imag * back_imag
            object_ref[1] += probe_real * back_imag - probe_imag * back_real
            win_real, win_imag = window_ref[0], window_ref[1]
            term_real = win_real * back_real + win_imag * back_imag
            term_imag = win_real * back_imag - win_imag * back_real
            if slot > 0:
                term_real += term_ref[0, mode]
                term_imag += term_ref[1, mode]
            if slot < slots - 1:
                term_ref[0, mode] = term_real
                term_ref[1, mode] = term_imag
            else:
                mine_ref[mode] = jnp.where(first, term_real, term_imag)
                other_ref[mode] = jnp.where(first, term_imag, term_real)
            return carry

        lax.fori_loop(0, modes, go_back, 0, unroll=UNROLL)
        for part in range(2):
            strip = jnp.concatenate(
                [object_ref[part], jnp.zeros((8, length), jnp.float32)], axis=0
            )
            strip = pltpu.roll(strip, shift, 0)
            strip = jnp.concatenate(
                [strip, jnp.zeros((length + 8, wide - length), jnp.float32)], axis=1
            )
            grad_ref[part, span, :] += pltpu.roll(strip, col, 1)


def device_gradients(place, block, above, below, left, right, probe, pattern):
    forward, backward = fourier_blocks(probe.shape[-1])
    _, modes, length, _ = probe.shape
    rows, cols = block.shape[1] + length, block.shape[2] + length
    slots = pattern.shape[0]
    vmem = pl.BlockSpec(memory_space=pltpu.VMEM)
    f32 = jnp.float32
    return pl.pallas_call(
        gradients_kernel,
        out_shape=(
            jax.ShapeDtypeStruct((2, rows, cols), f32),
            jax.ShapeDtypeStruct((modes, length, length), f32),
            jax.ShapeDtypeStruct((modes, length, length), f32),
        ),
        in_specs=[pl.BlockSpec(memory_space=pltpu.SMEM)] + [vmem] * 9,
        out_specs=(vmem, vmem, vmem),
        scratch_shapes=[
            pltpu.VMEM((2, rows, cols), f32),
            pltpu.VMEM((2, length, length), f32),
            pltpu.VMEM((modes, length, 2 * length), f32),
            pltpu.VMEM((length, length), f32),
            pltpu.VMEM((2, length, length), f32),
            pltpu.VMEM((2, modes, length, length), f32),
        ],
        compiler_params=pltpu.CompilerParams(vmem_limit_bytes=48 * 1024 * 1024),
        cost_estimate=pl.CostEstimate(
            flops=slots * modes * 32 * length**3, bytes_accessed=16 * 2**20, transcendentals=0
        ),
    )(place, block, above, below, left, right, probe, pattern, forward, backward)


def return_rims(grad_field, half_width):
    cols_rim = jnp.concatenate(
        [grad_field[:, :, :half_width], grad_field[:, :, -half_width:]], axis=2
    )
    cols_ext = padded_2(cols_rim, (("scan", 2),), half_width)
    core_block = grad_field[:, :, half_width:-half_width]
    core_block = core_block.at[:, :, :half_width].add(cols_ext[:, :, :half_width])
    core_block = core_block.at[:, :, -half_width:].add(cols_ext[:, :, -half_width:])
    rows_rim = jnp.concatenate([core_block[:, :half_width], core_block[:, -half_width:]], axis=1)
    rows_ext = padded_2(rows_rim, (("region", 1),), half_width)
    inner_block = core_block[:, half_width:-half_width]
    inner_block = inner_block.at[:, :half_width].add(rows_ext[:, :half_width])
    inner_block = inner_block.at[:, -half_width:].add(rows_ext[:, -half_width:])
    return inner_block


def axis_groups(kept):
    rows, cols = lax.axis_size("region"), lax.axis_size("scan")
    sizes = {"z": rows // 4, "y": 4, "x": cols // 2, "core": 2}
    groups = {}
    for device in range(rows * cols):
        place, rest = {}, device
        for name in ("core", "x", "y", "z"):
            place[name] = rest % sizes[name]
            rest = rest // sizes[name]
        key = tuple(place[name] for name in place if name not in kept)
        groups.setdefault(key, []).append(device)
    return [groups[key] for key in sorted(groups)]


def narrow(values, scale):
    return (values * (1.0 / scale)).astype(jnp.float16)


def widen(values, scale):
    return values.astype(jnp.float32) * scale


def exchange(parts, kept):
    return lax.all_to_all(parts, ("region", "scan"), 0, 0, axis_index_groups=axis_groups(kept))


def swap_cores(values):
    count = lax.axis_size("region") * lax.axis_size("scan")
    return lax.ppermute(values, ("region", "scan"), [(i, i ^ 1) for i in range(count)])


def sum_everywhere(mine, other):
    modes, rows, cols = mine.shape
    core = lax.axis_index("scan") % 2
    pair = mine + widen(swap_cores(narrow(other, 8.0)), 8.0)
    plane = 16
    slab = modes * rows // plane
    pieces = exchange(narrow(pair, 16.0).reshape(plane, slab, cols), ("y", "x"))
    slab_sum = jnp.sum(widen(pieces, 16.0), axis=0)
    depth = lax.axis_size("region") // 4
    pieces = exchange(slab_sum.reshape(depth, slab // depth, cols), ("z",))
    total = narrow(jnp.sum(pieces, axis=0), 2048.0)
    total = exchange(jnp.broadcast_to(total, (depth, slab // depth, cols)), ("z",))
    total = exchange(jnp.broadcast_to(total.reshape(slab, cols), (plane, slab, cols)), ("y", "x"))
    total = total.reshape(modes, rows, cols)
    swapped = swap_cores(total)
    first = core == 0
    return widen(
        jnp.stack([jnp.where(first, total, swapped), jnp.where(first, swapped, total)]), 2048.0
    )


def edges(cells, axis, dim, width):
    count = lax.axis_size(axis)
    ends = count - 1
    head = lax.slice_in_dim(cells, 0, width, axis=dim)
    tail = lax.slice_in_dim(cells, cells.shape[dim] - width, cells.shape[dim], axis=dim)
    before = lax.ppermute(tail, axis, [(i, (i + 1) % count) for i in range(ends)])
    after = lax.ppermute(head, axis, [((i + 1) % count, i) for i in range(ends)])
    return (before, after)


def on_device(object_field, probe_modes, pattern, rows_at, cols_at, object_step, probe_step):
    half_width = probe_modes.shape[-1] // 2
    block_rows = object_field.shape[1]
    block_cols = object_field.shape[2]
    core = lax.axis_index("scan") % 2
    place = jnp.stack(
        [
            rows_at[0, 0] % block_rows,
            cols_at[0, 0] % block_cols,
            jnp.broadcast_to(core, rows_at.shape[2:]).astype(jnp.int32),
        ]
    )
    cells = object_field.astype(jnp.bfloat16)
    above, below = edges(cells, "region", 1, half_width)
    tall = jnp.concatenate([above, cells, below], axis=1)
    left, right = edges(tall, "scan", 2, half_width)
    grad_field, mine, other = device_gradients(
        place, object_field, above, below, left, right, probe_modes, pattern[0, 0]
    )
    probe_total = sum_everywhere(mine, other)
    grad_block = return_rims(grad_field, half_width)
    object_field = object_field - object_step[0] * grad_block
    probe_modes = probe_modes - probe_step[0] * probe_total
    return (object_field, probe_modes)


def solution(mesh):
    return jax.shard_map(
        on_device,
        mesh=mesh,
        in_specs=(
            P(None, "region", "scan"),
            P(),
            P("region", "scan", None, None, None),
            P("region", "scan", None),
            P("region", "scan", None),
            P(),
            P(),
        ),
        out_specs=(P(None, "region", "scan"), P()),
        check_vma=False,
    )
```

```python
import math

import jax
import jax.numpy as jnp
import ml_dtypes
import numpy as np
from jax import lax
from jax.experimental import pallas as pl
from jax.experimental.pallas import tpu as pltpu
from jax.sharding import PartitionSpec as P


UNROLL = 8
GRANT = 52


def padded_2(cells, sides, width):
    for axis, dim in sides:
        count = lax.axis_size(axis)
        ends = count - 1
        head = lax.slice_in_dim(cells, 0, width, axis=dim)
        tail = lax.slice_in_dim(cells, cells.shape[dim] - width, cells.shape[dim], axis=dim)
        cells = jnp.concatenate(
            [
                lax.ppermute(tail, axis, [(i, (i + 1) % count) for i in range(ends)]),
                cells,
                lax.ppermute(head, axis, [((i + 1) % count, i) for i in range(ends)]),
            ],
            axis=dim,
        )
    return cells


def fourier_blocks(length):
    position = np.arange(length)
    angles = (position[:, None] * position[None, :] % length) * (2.0 * math.pi / length)
    table_scale = 1.0 / math.sqrt(length)
    cosine_table = (np.cos(angles) * table_scale).astype(ml_dtypes.bfloat16)
    sine_table = (np.sin(angles) * table_scale).astype(ml_dtypes.bfloat16)
    forward = np.block([[cosine_table, sine_table], [-sine_table, cosine_table]])
    return (jnp.asarray(forward), jnp.asarray(np.ascontiguousarray(forward.T)))


def fourier_pass(wide, left, right):
    length = wide.shape[0] // 2
    middle = jnp.dot(left, wide, preferred_element_type=jnp.float32).astype(jnp.bfloat16)
    middle = jnp.concatenate(
        [
            jnp.concatenate([middle[:length, cut], middle[length:, cut]], axis=1)
            for cut in (slice(i, i + length) for i in range(0, wide.shape[1], length))
        ],
        axis=0,
    )
    return jnp.dot(middle, right, preferred_element_type=jnp.float32)


def stacked(pairs):
    return jnp.concatenate(
        [jnp.concatenate(pair, axis=0).astype(jnp.bfloat16) for pair in pairs], axis=1
    )


def gradients_kernel(
    place_ref,
    block_hbm,
    above_hbm,
    below_hbm,
    left_hbm,
    right_hbm,
    probe_hbm,
    pattern_hbm,
    forward_hbm,
    backward_hbm,
    rim_left_hbm,
    center_hbm,
    rim_right_hbm,
    mine_hbm,
    other_hbm,
    block_ref,
    above_ref,
    below_ref,
    left_ref,
    right_ref,
    probe_ref,
    pattern_ref,
    forward_ref,
    backward_ref,
    rim_left_ref,
    center_ref,
    rim_right_ref,
    mine_ref,
    other_ref,
    padded_ref,
    window_ref,
    far_ref,
    level_ref,
    object_ref,
    probe_sem,
    piece_sem,
    mine_sem,
    other_sem,
    grad_sem,
):
    modes, length = probe_ref.shape[1], probe_ref.shape[2]
    half = length // 2
    rows, cols = block_ref.shape[1], block_ref.shape[2]
    wide = padded_ref.shape[2]
    slots = pattern_ref.shape[0]

    def fetch_probe(mode):
        return pltpu.make_async_copy(
            probe_hbm.at[:, mode], probe_ref.at[:, mode], probe_sem.at[mode]
        )

    def send_mine(mode):
        return pltpu.make_async_copy(mine_ref.at[mode], mine_hbm.at[mode], mine_sem.at[mode])

    def send_other(mode):
        return pltpu.make_async_copy(other_ref.at[mode], other_hbm.at[mode], other_sem.at[mode])

    fetches = [
        pltpu.make_async_copy(source, target, piece_sem.at[index])
        for index, (source, target) in enumerate(
            (
                (left_hbm, left_ref),
                (right_hbm, right_ref),
                (above_hbm, above_ref),
                (below_hbm, below_ref),
                (block_hbm, block_ref),
                (forward_hbm, forward_ref),
                (backward_hbm, backward_ref),
                (pattern_hbm, pattern_ref),
            )
        )
    ]
    for fetch in fetches:
        fetch.start()
    for mode in range(modes):
        fetch_probe(mode).start()
    for part_ref in (rim_left_ref, center_ref, rim_right_ref, level_ref, object_ref):
        part_ref[...] = jnp.zeros_like(part_ref)
    for fetch in fetches[:5]:
        fetch.wait()
    padded_ref[:, :, :half] = left_ref[...].astype(jnp.float32)
    padded_ref[:, :, half + cols :] = right_ref[...].astype(jnp.float32)
    padded_ref[:, :half, half : half + cols] = above_ref[...].astype(jnp.float32)
    padded_ref[:, half + rows :, half : half + cols] = below_ref[...].astype(jnp.float32)
    padded_ref[:, half : half + rows, half : half + cols] = (
        block_ref[...].astype(jnp.bfloat16).astype(jnp.float32)
    )
    first = place_ref[2, 0] == 0
    places = []
    for slot in range(slots):
        row, col = place_ref[0, slot], place_ref[1, slot]
        shift = row % 8
        span = pl.ds(pl.multiple_of(row - shift, 8), length + 8)
        places.append((span, shift, col))
        for part in range(2):
            strip = pltpu.roll(padded_ref[part, span, :], wide - col, 1)[:, :length]
            window_ref[slot, part] = pltpu.roll(strip, length + 8 - shift, 0)[:length]
    for fetch in fetches[5:]:
        fetch.wait()

    def go_forward(mode, carry):
        fetch_probe(mode).wait()
        probe_real, probe_imag = probe_ref[0, mode], probe_ref[1, mode]
        waves = []
        for slot in range(slots):
            win_real, win_imag = window_ref[slot, 0], window_ref[slot, 1]
            waves.append(
                (
                    probe_real * win_real - probe_imag * win_imag,
                    probe_real * win_imag + probe_imag * win_real,
                )
            )
        far = fourier_pass(stacked(waves), forward_ref[...], backward_ref[...])
        far_ref[mode] = far
        far_real, far_imag = far[:, :length], far[:, length:]
        level_ref[...] += far_real * far_real + far_imag * far_imag
        return carry

    lax.fori_loop(0, modes, go_forward, 0, unroll=UNROLL)
    amplitude = jnp.maximum(jnp.sqrt(level_ref[...]), 1.0)
    targets = jnp.concatenate([pattern_ref[slot] for slot in range(slots)], axis=0)
    level_ref[...] = 1.0 - jnp.sqrt(targets) / amplitude

    def go_back(mode, carry):
        corrected = []
        for slot in range(slots):
            band = slice(slot * length, (slot + 1) * length)
            factor = level_ref[band]
            far = far_ref[mode, band]
            corrected.append((factor * far[:, :length], factor * far[:, length:]))
        back = fourier_pass(stacked(corrected), backward_ref[...], forward_ref[...])
        probe_real, probe_imag = probe_ref[0, mode], probe_ref[1, mode]
        term_real = term_imag = 0.0
        for slot in range(slots):
            band = slice(slot * length, (slot + 1) * length)
            back_real, back_imag = back[band, :length], back[band, length:]
            object_ref[slot, 0] += probe_real * back_real + probe_imag * back_imag
            object_ref[slot, 1] += probe_real * back_imag - probe_imag * back_real
            win_real, win_imag = window_ref[slot, 0], window_ref[slot, 1]
            term_real += win_real * back_real + win_imag * back_imag
            term_imag += win_real * back_imag - win_imag * back_real
        mine_ref[mode] = jnp.where(first, term_real, term_imag)
        other_ref[mode] = jnp.where(first, term_imag, term_real)
        send_other(mode).start()
        send_mine(mode).start()
        return carry

    lax.fori_loop(0, modes, go_back, 0, unroll=UNROLL)
    for slot in range(slots):
        span, shift, col = places[slot]
        for part in range(2):
            strip = jnp.concatenate(
                [object_ref[slot, part], jnp.zeros((8, length), jnp.float32)], axis=0
            )
            strip = pltpu.roll(strip, shift, 0)
            strip = jnp.concatenate(
                [strip, jnp.zeros((length + 8, wide - length), jnp.float32)], axis=1
            )
            strip = pltpu.roll(strip, col, 1)
            rim_left_ref[part, span, :] += strip[:, :half]
            center_ref[part, span, :] += strip[:, half : half + cols]
            rim_right_ref[part, span, :] += strip[:, half + cols :]
    sends = [
        pltpu.make_async_copy(source, target, grad_sem.at[index])
        for index, (source, target) in enumerate(
            (
                (rim_left_ref, rim_left_hbm),
                (center_ref, center_hbm),
                (rim_right_ref, rim_right_hbm),
            )
        )
    ]
    for send in sends:
        send.start()
    for mode in range(modes):
        send_other(mode).wait()
        send_mine(mode).wait()
    for send in sends:
        send.wait()


def device_gradients(place, block, above, below, left, right, probe, pattern):
    forward, backward = fourier_blocks(probe.shape[-1])
    _, modes, length, _ = probe.shape
    rows, cols = block.shape[1] + length, block.shape[2] + length
    slots = pattern.shape[0]
    anywhere = pl.BlockSpec(memory_space=pl.ANY)
    f32 = jnp.float32
    fetched = (block, above, below, left, right, probe, pattern, forward, backward)
    made = (
        jax.ShapeDtypeStruct((2, rows, length // 2), f32),
        jax.ShapeDtypeStruct((2, rows, block.shape[2]), f32),
        jax.ShapeDtypeStruct((2, rows, length // 2), f32),
        jax.ShapeDtypeStruct((modes, length, length), f32),
        jax.ShapeDtypeStruct((modes, length, length), f32),
    )
    return pl.pallas_call(
        gradients_kernel,
        out_shape=made,
        in_specs=[pl.BlockSpec(memory_space=pltpu.SMEM)] + [anywhere] * len(fetched),
        out_specs=(anywhere,) * len(made),
        scratch_shapes=[pltpu.VMEM(item.shape, item.dtype) for item in fetched + made]
        + [
            pltpu.VMEM((2, rows, cols), f32),
            pltpu.VMEM((slots, 2, length, length), f32),
            pltpu.VMEM((modes, slots * length, 2 * length), f32),
            pltpu.VMEM((slots * length, length), f32),
            pltpu.VMEM((slots, 2, length, length), f32),
            pltpu.SemaphoreType.DMA((modes,)),
            pltpu.SemaphoreType.DMA((8,)),
            pltpu.SemaphoreType.DMA((modes,)),
            pltpu.SemaphoreType.DMA((modes,)),
            pltpu.SemaphoreType.DMA((3,)),
        ],
        compiler_params=pltpu.CompilerParams(vmem_limit_bytes=GRANT * 1024 * 1024),
        cost_estimate=pl.CostEstimate(
            flops=slots * modes * 32 * length**3, bytes_accessed=16 * 2**20, transcendentals=0
        ),
    )(place, *fetched)


def axis_groups(kept):
    rows, cols = lax.axis_size("region"), lax.axis_size("scan")
    sizes = {"core": 2, "x": cols // 2, "y": 4, "pair": 2, "far": rows // 8}
    groups = {}
    for device in range(rows * cols):
        place, rest = {}, device
        for name in sizes:
            place[name] = rest % sizes[name]
            rest = rest // sizes[name]
        key = tuple(place[name] for name in place if name not in kept)
        groups.setdefault(key, []).append(device)
    return [groups[key] for key in sorted(groups)]


def narrow(values, scale):
    return (values * (1.0 / scale)).astype(jnp.float16)


def widen(values, scale):
    return values.astype(jnp.float32) * scale


def exchange(parts, kept):
    return lax.all_to_all(parts, ("region", "scan"), 0, 0, axis_index_groups=axis_groups(kept))


def swap_cores(values):
    count = lax.axis_size("region") * lax.axis_size("scan")
    return lax.ppermute(values, ("region", "scan"), [(i, i ^ 1) for i in range(count)])


def shift_far(values, step):
    cols = lax.axis_size("scan")
    count = lax.axis_size("region") * cols
    stride = 8 * cols
    pairs = [(i, (i + step * stride) % count) for i in range(count)]
    return lax.ppermute(values, ("region", "scan"), pairs)


def sum_scattered(mine, other):
    modes, rows, cols = mine.shape
    pair = mine + widen(swap_cores(narrow(other, 8.0)), 8.0)
    places = 8 * (lax.axis_size("scan") // 2)
    pieces = narrow(pair, 16.0).reshape(places, modes * rows // places, cols)
    pieces = exchange(pieces, ("pair", "y", "x"))
    return jnp.sum(widen(pieces, 16.0), axis=0)


def sum_far(piece):
    sent = narrow(piece, 512.0)
    one, two, three = (widen(shift_far(sent, step), 512.0) for step in (1, 2, 3))
    return (widen(sent, 512.0) + two) + (one + three)


def gather_sum(total, modes):
    rows, cols = total.shape
    places = 8 * (lax.axis_size("scan") // 2)
    pieces = jnp.broadcast_to(narrow(total, 2048.0), (places, rows, cols))
    return exchange(pieces, ("pair", "y", "x")).reshape(modes, -1, cols)


def neighbours(head, tail, axis):
    count = lax.axis_size(axis)
    ends = count - 1
    before = lax.ppermute(tail, axis, [(i, (i + 1) % count) for i in range(ends)])
    after = lax.ppermute(head, axis, [((i + 1) % count, i) for i in range(ends)])
    return (before, after)


def edges(cells, axis, dim, width):
    head = lax.slice_in_dim(cells, 0, width, axis=dim)
    tail = lax.slice_in_dim(cells, cells.shape[dim] - width, cells.shape[dim], axis=dim)
    return neighbours(head, tail, axis)


def trade(head, tail, axis):
    return neighbours(narrow(head, 64.0), narrow(tail, 64.0), axis)


def on_device(object_field, probe_modes, pattern, rows_at, cols_at, object_step, probe_step):
    half_width = probe_modes.shape[-1] // 2
    block_rows = object_field.shape[1]
    block_cols = object_field.shape[2]
    core = lax.axis_index("scan") % 2
    place = jnp.stack(
        [
            rows_at[0, 0] % block_rows,
            cols_at[0, 0] % block_cols,
            jnp.broadcast_to(core, rows_at.shape[2:]).astype(jnp.int32),
        ]
    )
    cells = object_field.astype(jnp.bfloat16)
    above, below = edges(cells, "region", 1, half_width)
    tall = jnp.concatenate([above, cells, below], axis=1)
    left, right = edges(tall, "scan", 2, half_width)
    rim_left, center, rim_right, mine, other = device_gradients(
        place, object_field, above, below, left, right, probe_modes, pattern[0, 0]
    )
    piece = sum_scattered(mine, other)
    from_left, from_right = trade(rim_left, rim_right, "scan")
    center = center + widen(jnp.concatenate([from_left, from_right], axis=2), 64.0)
    piece, center = lax.optimization_barrier((piece, center))
    total = sum_far(piece)
    total, center = lax.optimization_barrier((total, center))
    from_above, from_below = trade(center[:, :half_width], center[:, -half_width:], "region")
    plane = gather_sum(total, probe_modes.shape[1])
    plane, from_above, from_below = lax.optimization_barrier((plane, from_above, from_below))
    swapped = swap_cores(plane)
    inner = center[:, half_width:-half_width]
    inner = inner + widen(jnp.concatenate([from_above, from_below], axis=1), 64.0)
    object_field = object_field - object_step[0] * inner
    own = lax.broadcasted_iota(jnp.int32, probe_modes.shape, 0) == core
    probe_total = widen(jnp.where(own, plane[None], swapped[None]), 2048.0)
    probe_modes = probe_modes - probe_step[0] * probe_total
    return (object_field, probe_modes)


def solution(mesh):
    return jax.shard_map(
        on_device,
        mesh=mesh,
        in_specs=(
            P(None, "region", "scan"),
            P(),
            P("region", "scan", None, None, None),
            P("region", "scan", None),
            P("region", "scan", None),
            P(),
            P(),
        ),
        out_specs=(P(None, "region", "scan"), P()),
        check_vma=False,
    )
```

```python
import math

import jax
import jax.numpy as jnp
import ml_dtypes
import numpy as np
from jax import lax
from jax.experimental import pallas as pl
from jax.experimental.pallas import tpu as pltpu
from jax.sharding import PartitionSpec as P


UNROLL = 8
GRANT = 52


def padded_2(cells, sides, width):
    for axis, dim in sides:
        count = lax.axis_size(axis)
        ends = count - 1
        head = lax.slice_in_dim(cells, 0, width, axis=dim)
        tail = lax.slice_in_dim(cells, cells.shape[dim] - width, cells.shape[dim], axis=dim)
        cells = jnp.concatenate(
            [
                lax.ppermute(tail, axis, [(i, (i + 1) % count) for i in range(ends)]),
                cells,
                lax.ppermute(head, axis, [((i + 1) % count, i) for i in range(ends)]),
            ],
            axis=dim,
        )
    return cells


def fourier_blocks(length):
    position = np.arange(length)
    angles = (position[:, None] * position[None, :] % length) * (2.0 * math.pi / length)
    table_scale = 1.0 / math.sqrt(length)
    cosine_table = (np.cos(angles) * table_scale).astype(ml_dtypes.bfloat16)
    sine_table = (np.sin(angles) * table_scale).astype(ml_dtypes.bfloat16)
    forward = np.block([[cosine_table, sine_table], [-sine_table, cosine_table]])
    return (jnp.asarray(forward), jnp.asarray(np.ascontiguousarray(forward.T)))


def fourier_pass(wide, left, right):
    length = wide.shape[0] // 2
    middle = jnp.dot(left, wide, preferred_element_type=jnp.float32).astype(jnp.bfloat16)
    middle = jnp.concatenate(
        [
            jnp.concatenate([middle[:length, cut], middle[length:, cut]], axis=1)
            for cut in (slice(i, i + length) for i in range(0, wide.shape[1], length))
        ],
        axis=0,
    )
    return jnp.dot(middle, right, preferred_element_type=jnp.float32)


def stacked(pairs):
    return jnp.concatenate(
        [jnp.concatenate(pair, axis=0).astype(jnp.bfloat16) for pair in pairs], axis=1
    )


def gradients_kernel(
    place_ref,
    block_hbm,
    above_hbm,
    below_hbm,
    left_hbm,
    right_hbm,
    probe_hbm,
    pattern_hbm,
    forward_hbm,
    backward_hbm,
    rim_left_hbm,
    center_hbm,
    rim_right_hbm,
    mine_hbm,
    other_hbm,
    block_ref,
    above_ref,
    below_ref,
    left_ref,
    right_ref,
    probe_ref,
    pattern_ref,
    forward_ref,
    backward_ref,
    rim_left_ref,
    center_ref,
    rim_right_ref,
    mine_ref,
    other_ref,
    padded_ref,
    window_ref,
    far_ref,
    level_ref,
    object_ref,
    probe_sem,
    piece_sem,
    mine_sem,
    other_sem,
    grad_sem,
):
    modes, length = probe_ref.shape[1], probe_ref.shape[2]
    half = length // 2
    rows, cols = block_ref.shape[1], block_ref.shape[2]
    wide = padded_ref.shape[2]
    slots = pattern_ref.shape[0]

    def fetch_probe(mode):
        return pltpu.make_async_copy(
            probe_hbm.at[:, mode], probe_ref.at[:, mode], probe_sem.at[mode]
        )

    def send_mine(mode):
        return pltpu.make_async_copy(mine_ref.at[mode], mine_hbm.at[mode], mine_sem.at[mode])

    def send_other(mode):
        return pltpu.make_async_copy(other_ref.at[mode], other_hbm.at[mode], other_sem.at[mode])

    fetches = [
        pltpu.make_async_copy(source, target, piece_sem.at[index])
        for index, (source, target) in enumerate(
            (
                (left_hbm, left_ref),
                (right_hbm, right_ref),
                (above_hbm, above_ref),
                (below_hbm, below_ref),
                (block_hbm, block_ref),
                (forward_hbm, forward_ref),
                (backward_hbm, backward_ref),
                (pattern_hbm, pattern_ref),
            )
        )
    ]
    for fetch in fetches:
        fetch.start()
    for mode in range(modes):
        fetch_probe(mode).start()
    for part_ref in (rim_left_ref, center_ref, rim_right_ref, level_ref, object_ref):
        part_ref[...] = jnp.zeros_like(part_ref)
    for fetch in fetches[:5]:
        fetch.wait()
    padded_ref[:, :, :half] = left_ref[...].astype(jnp.float32)
    padded_ref[:, :, half + cols :] = right_ref[...].astype(jnp.float32)
    padded_ref[:, :half, half : half + cols] = above_ref[...].astype(jnp.float32)
    padded_ref[:, half + rows :, half : half + cols] = below_ref[...].astype(jnp.float32)
    padded_ref[:, half : half + rows, half : half + cols] = (
        block_ref[...].astype(jnp.bfloat16).astype(jnp.float32)
    )
    first = place_ref[2, 0] == 0
    places = []
    for slot in range(slots):
        row, col = place_ref[0, slot], place_ref[1, slot]
        shift = row % 8
        span = pl.ds(pl.multiple_of(row - shift, 8), length + 8)
        places.append((span, shift, col))
        for part in range(2):
            strip = pltpu.roll(padded_ref[part, span, :], wide - col, 1)[:, :length]
            window_ref[slot, part] = pltpu.roll(strip, length + 8 - shift, 0)[:length]
    for fetch in fetches[5:]:
        fetch.wait()

    def go_forward(mode, carry):
        fetch_probe(mode).wait()
        probe_real, probe_imag = probe_ref[0, mode], probe_ref[1, mode]
        waves = []
        for slot in range(slots):
            win_real, win_imag = window_ref[slot, 0], window_ref[slot, 1]
            waves.append(
                (
                    probe_real * win_real - probe_imag * win_imag,
                    probe_real * win_imag + probe_imag * win_real,
                )
            )
        far = fourier_pass(stacked(waves), forward_ref[...], backward_ref[...])
        far_ref[mode] = far
        far_real, far_imag = far[:, :length], far[:, length:]
        level_ref[...] += far_real * far_real + far_imag * far_imag
        return carry

    lax.fori_loop(0, modes, go_forward, 0, unroll=UNROLL)
    amplitude = jnp.maximum(jnp.sqrt(level_ref[...]), 1.0)
    targets = jnp.concatenate([pattern_ref[slot] for slot in range(slots)], axis=0)
    level_ref[...] = 1.0 - jnp.sqrt(targets) / amplitude

    def go_back(mode, carry):
        corrected = []
        for slot in range(slots):
            band = slice(slot * length, (slot + 1) * length)
            factor = level_ref[band]
            far = far_ref[mode, band]
            corrected.append((factor * far[:, :length], factor * far[:, length:]))
        back = fourier_pass(stacked(corrected), backward_ref[...], forward_ref[...])
        probe_real, probe_imag = probe_ref[0, mode], probe_ref[1, mode]
        term_real = term_imag = 0.0
        for slot in range(slots):
            band = slice(slot * length, (slot + 1) * length)
            back_real, back_imag = back[band, :length], back[band, length:]
            object_ref[slot, 0] += probe_real * back_real + probe_imag * back_imag
            object_ref[slot, 1] += probe_real * back_imag - probe_imag * back_real
            win_real, win_imag = window_ref[slot, 0], window_ref[slot, 1]
            term_real += win_real * back_real + win_imag * back_imag
            term_imag += win_real * back_imag - win_imag * back_real
        mine_ref[mode] = jnp.where(first, term_real, term_imag)
        other_ref[mode] = jnp.where(first, term_imag, term_real)
        send_other(mode).start()
        send_mine(mode).start()
        return carry

    lax.fori_loop(0, modes, go_back, 0, unroll=UNROLL)
    for slot in range(slots):
        span, shift, col = places[slot]
        for part in range(2):
            strip = jnp.concatenate(
                [object_ref[slot, part], jnp.zeros((8, length), jnp.float32)], axis=0
            )
            strip = pltpu.roll(strip, shift, 0)
            strip = jnp.concatenate(
                [strip, jnp.zeros((length + 8, wide - length), jnp.float32)], axis=1
            )
            strip = pltpu.roll(strip, col, 1)
            rim_left_ref[part, span, :] += strip[:, :half]
            center_ref[part, span, :] += strip[:, half : half + cols]
            rim_right_ref[part, span, :] += strip[:, half + cols :]
    sends = [
        pltpu.make_async_copy(source, target, grad_sem.at[index])
        for index, (source, target) in enumerate(
            (
                (rim_left_ref, rim_left_hbm),
                (center_ref, center_hbm),
                (rim_right_ref, rim_right_hbm),
            )
        )
    ]
    for send in sends:
        send.start()
    for mode in range(modes):
        send_other(mode).wait()
        send_mine(mode).wait()
    for send in sends:
        send.wait()


def device_gradients(place, block, above, below, left, right, probe, pattern):
    forward, backward = fourier_blocks(probe.shape[-1])
    _, modes, length, _ = probe.shape
    rows, cols = block.shape[1] + length, block.shape[2] + length
    slots = pattern.shape[0]
    anywhere = pl.BlockSpec(memory_space=pl.ANY)
    f32 = jnp.float32
    fetched = (block, above, below, left, right, probe, pattern, forward, backward)
    made = (
        jax.ShapeDtypeStruct((2, rows, length // 2), f32),
        jax.ShapeDtypeStruct((2, rows, block.shape[2]), f32),
        jax.ShapeDtypeStruct((2, rows, length // 2), f32),
        jax.ShapeDtypeStruct((modes, length, length), f32),
        jax.ShapeDtypeStruct((modes, length, length), f32),
    )
    return pl.pallas_call(
        gradients_kernel,
        out_shape=made,
        in_specs=[pl.BlockSpec(memory_space=pltpu.SMEM)] + [anywhere] * len(fetched),
        out_specs=(anywhere,) * len(made),
        scratch_shapes=[pltpu.VMEM(item.shape, item.dtype) for item in fetched + made]
        + [
            pltpu.VMEM((2, rows, cols), f32),
            pltpu.VMEM((slots, 2, length, length), f32),
            pltpu.VMEM((modes, slots * length, 2 * length), f32),
            pltpu.VMEM((slots * length, length), f32),
            pltpu.VMEM((slots, 2, length, length), f32),
            pltpu.SemaphoreType.DMA((modes,)),
            pltpu.SemaphoreType.DMA((8,)),
            pltpu.SemaphoreType.DMA((modes,)),
            pltpu.SemaphoreType.DMA((modes,)),
            pltpu.SemaphoreType.DMA((3,)),
        ],
        compiler_params=pltpu.CompilerParams(vmem_limit_bytes=GRANT * 1024 * 1024),
        cost_estimate=pl.CostEstimate(
            flops=slots * modes * 32 * length**3, bytes_accessed=16 * 2**20, transcendentals=0
        ),
    )(place, *fetched)


def axis_groups(kept):
    rows, cols = lax.axis_size("region"), lax.axis_size("scan")
    sizes = {"core": 2, "x": cols // 2, "y": 4, "pair": 2, "far": rows // 8}
    groups = {}
    for device in range(rows * cols):
        place, rest = {}, device
        for name in sizes:
            place[name] = rest % sizes[name]
            rest = rest // sizes[name]
        key = tuple(place[name] for name in place if name not in kept)
        groups.setdefault(key, []).append(device)
    return [groups[key] for key in sorted(groups)]


def narrow(values, scale):
    return (values * (1.0 / scale)).astype(jnp.float16)


def widen(values, scale):
    return values.astype(jnp.float32) * scale


def exchange(parts, kept):
    return lax.all_to_all(parts, ("region", "scan"), 0, 0, axis_index_groups=axis_groups(kept))


def swap_cores(values):
    count = lax.axis_size("region") * lax.axis_size("scan")
    return lax.ppermute(values, ("region", "scan"), [(i, i ^ 1) for i in range(count)])


def shift_far(values, step):
    cols = lax.axis_size("scan")
    count = lax.axis_size("region") * cols
    stride = 8 * cols
    pairs = [(i, (i + step * stride) % count) for i in range(count)]
    return lax.ppermute(values, ("region", "scan"), pairs)


def sum_scattered(mine, other):
    modes, rows, cols = mine.shape
    pair = mine + widen(swap_cores(narrow(other, 8.0)), 8.0)
    places = 8 * (lax.axis_size("scan") // 2)
    pieces = narrow(pair, 16.0).reshape(places, modes * rows // places, cols)
    pieces = exchange(pieces, ("pair", "y", "x"))
    return jnp.sum(widen(pieces, 16.0), axis=0)


def sum_far(piece):
    sent = narrow(piece, 512.0)
    one, two, three = (widen(shift_far(sent, step), 512.0) for step in (1, 2, 3))
    return (widen(sent, 512.0) + two) + (one + three)


def gather_all(total, modes):
    rows, cols = total.shape
    places = 8 * (lax.axis_size("scan") // 2)
    pieces = jnp.broadcast_to(total, (places, rows, cols))
    return exchange(pieces, ("pair", "y", "x")).reshape(modes, -1, cols)


def neighbours(head, tail, axis):
    count = lax.axis_size(axis)
    even = lax.axis_index(axis) % 2 == 0
    swaps = [
        [pair for i in range(start, count - 1, 2) for pair in ((i, i + 1), (i + 1, i))]
        for start in (0, 1)
    ]
    inner = lax.ppermute(jnp.where(even, tail, head), axis, swaps[0])
    outer = lax.ppermute(jnp.where(even, head, tail), axis, swaps[1])
    return (jnp.where(even, outer, inner), jnp.where(even, inner, outer))


def edges(cells, axis, dim, width):
    head = lax.slice_in_dim(cells, 0, width, axis=dim)
    tail = lax.slice_in_dim(cells, cells.shape[dim] - width, cells.shape[dim], axis=dim)
    return neighbours(head, tail, axis)


def trade(head, tail, axis):
    return neighbours(narrow(head, 64.0), narrow(tail, 64.0), axis)


def on_device(object_field, probe_modes, pattern, rows_at, cols_at, object_step, probe_step):
    half_width = probe_modes.shape[-1] // 2
    block_rows = object_field.shape[1]
    block_cols = object_field.shape[2]
    core = lax.axis_index("scan") % 2
    place = jnp.stack(
        [
            rows_at[0, 0] % block_rows,
            cols_at[0, 0] % block_cols,
            jnp.broadcast_to(core, rows_at.shape[2:]).astype(jnp.int32),
        ]
    )
    cells = object_field.astype(jnp.bfloat16)
    above, below = edges(cells, "region", 1, half_width)
    tall = jnp.concatenate([above, cells, below], axis=1)
    left, right = edges(tall, "scan", 2, half_width)
    rim_left, center, rim_right, mine, other = device_gradients(
        place, object_field, above, below, left, right, probe_modes, pattern[0, 0]
    )
    piece = sum_scattered(mine, other)
    from_left, from_right = trade(rim_left, rim_right, "scan")
    center = center + widen(jnp.concatenate([from_left, from_right], axis=2), 64.0)
    piece, center = lax.optimization_barrier((piece, center))
    total = sum_far(piece)
    region, scan = lax.axis_index("region"), lax.axis_index("scan")
    spot = (region % 8 * 4 + scan // 2) * total.shape[0]
    flat = probe_modes.reshape(2, -1, probe_modes.shape[-1])
    mine = lax.dynamic_slice(flat, (core, spot, 0), (1, *total.shape))[0]
    updated = narrow(mine - probe_step[0] * total, 128.0)
    updated, center = lax.optimization_barrier((updated, center))
    from_above, from_below = trade(center[:, :half_width], center[:, -half_width:], "region")
    plane = gather_all(updated, probe_modes.shape[1])
    plane, from_above, from_below = lax.optimization_barrier((plane, from_above, from_below))
    swapped = swap_cores(plane)
    inner = center[:, half_width:-half_width]
    inner = inner + widen(jnp.concatenate([from_above, from_below], axis=1), 64.0)
    object_field = object_field - object_step[0] * inner
    own = lax.broadcasted_iota(jnp.int32, probe_modes.shape, 0) == core
    probe_modes = widen(jnp.where(own, plane[None], swapped[None]), 128.0)
    return (object_field, probe_modes)


def solution(mesh):
    return jax.shard_map(
        on_device,
        mesh=mesh,
        in_specs=(
            P(None, "region", "scan"),
            P(),
            P("region", "scan", None, None, None),
            P("region", "scan", None),
            P("region", "scan", None),
            P(),
            P(),
        ),
        out_specs=(P(None, "region", "scan"), P()),
        check_vma=False,
    )
```

```python
import math

import jax
import jax.numpy as jnp
import ml_dtypes
import numpy as np
from jax import lax
from jax.experimental import pallas as pl
from jax.experimental.pallas import tpu as pltpu
from jax.sharding import PartitionSpec as P


UNROLL = 8
GRANT = 42


def padded_2(cells, sides, width):
    for axis, dim in sides:
        count = lax.axis_size(axis)
        ends = count - 1
        head = lax.slice_in_dim(cells, 0, width, axis=dim)
        tail = lax.slice_in_dim(cells, cells.shape[dim] - width, cells.shape[dim], axis=dim)
        cells = jnp.concatenate(
            [
                lax.ppermute(tail, axis, [(i, (i + 1) % count) for i in range(ends)]),
                cells,
                lax.ppermute(head, axis, [((i + 1) % count, i) for i in range(ends)]),
            ],
            axis=dim,
        )
    return cells


def fourier_tables(length):
    position = np.arange(length)
    angles = (position[:, None] * position[None, :] % length) * (2.0 * math.pi / length)
    table_scale = 1.0 / math.sqrt(length)
    cosine_table = (np.cos(angles) * table_scale).astype(ml_dtypes.bfloat16)
    sine_table = (np.sin(angles) * table_scale).astype(ml_dtypes.bfloat16)
    return (jnp.asarray(cosine_table), jnp.asarray(sine_table))


def fourier_pass(wide, left, right):
    length = wide.shape[0] // 2
    middle = jnp.dot(left, wide, preferred_element_type=jnp.float32).astype(jnp.bfloat16)
    middle = jnp.concatenate(
        [
            jnp.concatenate([middle[:length, cut], middle[length:, cut]], axis=1)
            for cut in (slice(i, i + length) for i in range(0, wide.shape[1], length))
        ],
        axis=0,
    )
    return jnp.dot(middle, right, preferred_element_type=jnp.float32)


def stacked(pairs):
    return jnp.concatenate(
        [jnp.concatenate(pair, axis=0).astype(jnp.bfloat16) for pair in pairs], axis=1
    )


def gradients_kernel(
    place_ref,
    block_hbm,
    above_hbm,
    below_hbm,
    left_hbm,
    right_hbm,
    probe_hbm,
    pattern_hbm,
    cosine_hbm,
    sine_hbm,
    rim_left_ref,
    center_ref,
    rim_right_ref,
    mine_ref,
    other_ref,
    block_ref,
    above_ref,
    below_ref,
    left_ref,
    right_ref,
    probe_ref,
    pattern_ref,
    cosine_ref,
    sine_ref,
    forward_ref,
    backward_ref,
    padded_ref,
    window_ref,
    far_ref,
    level_ref,
    object_ref,
    probe_sem,
    piece_sem,
):
    modes, length = probe_ref.shape[1], probe_ref.shape[2]
    half = length // 2
    rows, cols = block_ref.shape[1], block_ref.shape[2]
    wide = padded_ref.shape[2]
    slots = pattern_ref.shape[0]

    def fetch_probe(mode):
        return pltpu.make_async_copy(
            probe_hbm.at[:, mode], probe_ref.at[:, mode], probe_sem.at[mode]
        )

    fetches = [
        pltpu.make_async_copy(source, target, piece_sem.at[index])
        for index, (source, target) in enumerate(
            (
                (left_hbm, left_ref),
                (right_hbm, right_ref),
                (above_hbm, above_ref),
                (below_hbm, below_ref),
                (block_hbm, block_ref),
                (cosine_hbm, cosine_ref),
                (sine_hbm, sine_ref),
                (pattern_hbm, pattern_ref),
            )
        )
    ]
    for fetch in fetches[5:7] + fetches[:5] + fetches[7:]:
        fetch.start()
    for mode in range(modes):
        fetch_probe(mode).start()
    for part_ref in (rim_left_ref, center_ref, rim_right_ref, level_ref, object_ref):
        part_ref[...] = jnp.zeros_like(part_ref)
    for fetch in fetches[5:7]:
        fetch.wait()
    low, high = slice(0, length), slice(length, 2 * length)
    cosine, sine = cosine_ref[...], sine_ref[...]
    for table_ref in (forward_ref, backward_ref):
        table_ref[low, low] = cosine
        table_ref[high, high] = cosine
    forward_ref[low, high] = sine
    backward_ref[high, low] = sine
    forward_ref[high, low] = -sine
    backward_ref[low, high] = -sine
    for fetch in fetches[:5]:
        fetch.wait()
    padded_ref[:, :, :half] = left_ref[...].astype(jnp.float32)
    padded_ref[:, :, half + cols :] = right_ref[...].astype(jnp.float32)
    padded_ref[:, :half, half : half + cols] = above_ref[...].astype(jnp.float32)
    padded_ref[:, half + rows :, half : half + cols] = below_ref[...].astype(jnp.float32)
    padded_ref[:, half : half + rows, half : half + cols] = (
        block_ref[...].astype(jnp.bfloat16).astype(jnp.float32)
    )
    first = place_ref[2, 0] == 0
    places = []
    for slot in range(slots):
        row, col = place_ref[0, slot], place_ref[1, slot]
        shift = row % 8
        span = pl.ds(pl.multiple_of(row - shift, 8), length + 8)
        places.append((span, shift, col))
        for part in range(2):
            strip = pltpu.roll(padded_ref[part, span, :], wide - col, 1)[:, :length]
            window_ref[slot, part] = pltpu.roll(strip, length + 8 - shift, 0)[:length]
    fetches[7].wait()

    def go_forward(mode, carry):
        fetch_probe(mode).wait()
        probe_real, probe_imag = probe_ref[0, mode], probe_ref[1, mode]
        waves = []
        for slot in range(slots):
            win_real, win_imag = window_ref[slot, 0], window_ref[slot, 1]
            waves.append(
                (
                    probe_real * win_real - probe_imag * win_imag,
                    probe_real * win_imag + probe_imag * win_real,
                )
            )
        far = fourier_pass(stacked(waves), forward_ref[...], backward_ref[...])
        far_ref[mode] = far
        far_real, far_imag = far[:, :length], far[:, length:]
        level_ref[...] += far_real * far_real + far_imag * far_imag
        return carry

    lax.fori_loop(0, modes, go_forward, 0, unroll=UNROLL)
    amplitude = jnp.maximum(jnp.sqrt(level_ref[...]), 1.0)
    targets = jnp.concatenate([pattern_ref[slot] for slot in range(slots)], axis=0)
    level_ref[...] = 1.0 - jnp.sqrt(targets) / amplitude

    def go_back(mode, carry):
        corrected = []
        for slot in range(slots):
            band = slice(slot * length, (slot + 1) * length)
            factor = level_ref[band]
            far = far_ref[mode, band]
            corrected.append((factor * far[:, :length], factor * far[:, length:]))
        back = fourier_pass(stacked(corrected), backward_ref[...], forward_ref[...])
        probe_real, probe_imag = probe_ref[0, mode], probe_ref[1, mode]
        term_real = term_imag = 0.0
        for slot in range(slots):
            band = slice(slot * length, (slot + 1) * length)
            back_real, back_imag = back[band, :length], back[band, length:]
            object_ref[slot, 0] += probe_real * back_real + probe_imag * back_imag
            object_ref[slot, 1] += probe_real * back_imag - probe_imag * back_real
            win_real, win_imag = window_ref[slot, 0], window_ref[slot, 1]
            term_real += win_real * back_real + win_imag * back_imag
            term_imag += win_real * back_imag - win_imag * back_real
        mine_ref[mode] = jnp.where(first, term_real, term_imag)
        other_ref[mode] = jnp.where(first, term_imag, term_real)
        return carry

    lax.fori_loop(0, modes, go_back, 0, unroll=UNROLL)
    for slot in range(slots):
        span, shift, col = places[slot]
        for part in range(2):
            strip = jnp.concatenate(
                [object_ref[slot, part], jnp.zeros((8, length), jnp.float32)], axis=0
            )
            strip = pltpu.roll(strip, shift, 0)
            strip = jnp.concatenate(
                [strip, jnp.zeros((length + 8, wide - length), jnp.float32)], axis=1
            )
            strip = pltpu.roll(strip, col, 1)
            rim_left_ref[part, span, :] += strip[:, :half]
            center_ref[part, span, :] += strip[:, half : half + cols]
            rim_right_ref[part, span, :] += strip[:, half + cols :]


def device_gradients(place, block, above, below, left, right, probe, pattern):
    cosine, sine = fourier_tables(probe.shape[-1])
    _, modes, length, _ = probe.shape
    rows, cols = block.shape[1] + length, block.shape[2] + length
    slots = pattern.shape[0]
    anywhere = pl.BlockSpec(memory_space=pl.ANY)
    f32 = jnp.float32
    fetched = (block, above, below, left, right, probe, pattern, cosine, sine)
    made = (
        jax.ShapeDtypeStruct((2, rows, length // 2), f32),
        jax.ShapeDtypeStruct((2, rows, block.shape[2]), f32),
        jax.ShapeDtypeStruct((2, rows, length // 2), f32),
        jax.ShapeDtypeStruct((modes, length, length), f32),
        jax.ShapeDtypeStruct((modes, length, length), f32),
    )
    return pl.pallas_call(
        gradients_kernel,
        out_shape=made,
        in_specs=[pl.BlockSpec(memory_space=pltpu.SMEM)] + [anywhere] * len(fetched),
        out_specs=(pl.BlockSpec(memory_space=pltpu.VMEM),) * len(made),
        scratch_shapes=[pltpu.VMEM(item.shape, item.dtype) for item in fetched]
        + [
            pltpu.VMEM((2 * length, 2 * length), jnp.bfloat16),
            pltpu.VMEM((2 * length, 2 * length), jnp.bfloat16),
            pltpu.VMEM((2, rows, cols), f32),
            pltpu.VMEM((slots, 2, length, length), f32),
            pltpu.VMEM((modes, slots * length, 2 * length), f32),
            pltpu.VMEM((slots * length, length), f32),
            pltpu.VMEM((slots, 2, length, length), f32),
            pltpu.SemaphoreType.DMA((modes,)),
            pltpu.SemaphoreType.DMA((8,)),
        ],
        compiler_params=pltpu.CompilerParams(vmem_limit_bytes=GRANT * 1024 * 1024),
        cost_estimate=pl.CostEstimate(
            flops=slots * modes * 32 * length**3, bytes_accessed=16 * 2**20, transcendentals=0
        ),
    )(place, *fetched)


def axis_groups(kept):
    rows, cols = lax.axis_size("region"), lax.axis_size("scan")
    sizes = {"core": 2, "x": cols // 2, "y": 4, "pair": 2, "far": rows // 8}
    groups = {}
    for device in range(rows * cols):
        place, rest = {}, device
        for name in sizes:
            place[name] = rest % sizes[name]
            rest = rest // sizes[name]
        key = tuple(place[name] for name in place if name not in kept)
        groups.setdefault(key, []).append(device)
    return [groups[key] for key in sorted(groups)]


def narrow(values, scale):
    return (values * (1.0 / scale)).astype(jnp.float16)


def widen(values, scale):
    return values.astype(jnp.float32) * scale


def exchange(parts, kept):
    return lax.all_to_all(parts, ("region", "scan"), 0, 0, axis_index_groups=axis_groups(kept))


def swap_cores(values):
    count = lax.axis_size("region") * lax.axis_size("scan")
    return lax.ppermute(values, ("region", "scan"), [(i, i ^ 1) for i in range(count)])


def shift_far(values, step):
    cols = lax.axis_size("scan")
    count = lax.axis_size("region") * cols
    stride = 8 * cols
    pairs = [(i, (i + step * stride) % count) for i in range(count)]
    return lax.ppermute(values, ("region", "scan"), pairs)


def sum_scattered(mine, other):
    modes, rows, cols = mine.shape
    pair = mine + widen(swap_cores(narrow(other, 8.0)), 8.0)
    places = 8 * (lax.axis_size("scan") // 2)
    pieces = narrow(pair, 16.0).reshape(places, modes * rows // places, cols)
    pieces = exchange(pieces, ("pair", "y", "x"))
    return jnp.sum(widen(pieces, 16.0), axis=0)


def sum_far(piece):
    sent = narrow(piece, 512.0)
    one, two, three = (widen(shift_far(sent, step), 512.0) for step in (1, 2, 3))
    return (widen(sent, 512.0) + two) + (one + three)


def gather_all(total, modes):
    rows, cols = total.shape
    places = 8 * (lax.axis_size("scan") // 2)
    pieces = jnp.broadcast_to(total, (places, rows, cols))
    return exchange(pieces, ("pair", "y", "x")).reshape(modes, -1, cols)


def neighbours(head, tail, axis):
    count = lax.axis_size(axis)
    even = lax.axis_index(axis) % 2 == 0
    swaps = [
        [pair for i in range(start, count - 1, 2) for pair in ((i, i + 1), (i + 1, i))]
        for start in (0, 1)
    ]
    inner = lax.ppermute(jnp.where(even, tail, head), axis, swaps[0])
    outer = lax.ppermute(jnp.where(even, head, tail), axis, swaps[1])
    return (jnp.where(even, outer, inner), jnp.where(even, inner, outer))


def edges(cells, axis, dim, width):
    head = lax.slice_in_dim(cells, 0, width, axis=dim)
    tail = lax.slice_in_dim(cells, cells.shape[dim] - width, cells.shape[dim], axis=dim)
    return neighbours(head, tail, axis)


def trade(head, tail, axis):
    return neighbours(narrow(head, 64.0), narrow(tail, 64.0), axis)


def on_device(object_field, probe_modes, pattern, rows_at, cols_at, object_step, probe_step):
    half_width = probe_modes.shape[-1] // 2
    block_rows = object_field.shape[1]
    block_cols = object_field.shape[2]
    core = lax.axis_index("scan") % 2
    place = jnp.stack(
        [
            rows_at[0, 0] % block_rows,
            cols_at[0, 0] % block_cols,
            jnp.broadcast_to(core, rows_at.shape[2:]).astype(jnp.int32),
        ]
    )
    cells = object_field.astype(jnp.bfloat16)
    above, below = edges(cells, "region", 1, half_width)
    tall = jnp.concatenate([above, cells, below], axis=1)
    left, right = edges(tall, "scan", 2, half_width)
    rim_left, center, rim_right, mine, other = device_gradients(
        place, object_field, above, below, left, right, probe_modes, pattern[0, 0]
    )
    piece = sum_scattered(mine, other)
    from_left, from_right = trade(rim_left, rim_right, "scan")
    center = center + widen(jnp.concatenate([from_left, from_right], axis=2), 64.0)
    piece, center = lax.optimization_barrier((piece, center))
    region, scan = lax.axis_index("region"), lax.axis_index("scan")
    spot = (region % 8 * 4 + scan // 2) * piece.shape[0]
    flat = probe_modes.reshape(2, -1, probe_modes.shape[-1])
    mine = lax.dynamic_slice(flat, (core, spot, 0), (1, *piece.shape))[0]
    piece, mine = lax.optimization_barrier((piece, mine))
    total = sum_far(piece)
    updated = narrow(mine - probe_step[0] * total, 128.0)
    updated, center = lax.optimization_barrier((updated, center))
    from_above, from_below = trade(center[:, :half_width], center[:, -half_width:], "region")
    plane = gather_all(updated, probe_modes.shape[1])
    plane, from_above, from_below = lax.optimization_barrier((plane, from_above, from_below))
    swapped = swap_cores(plane)
    inner = center[:, half_width:-half_width]
    inner = inner + widen(jnp.concatenate([from_above, from_below], axis=1), 64.0)
    object_field = object_field - object_step[0] * inner
    own = lax.broadcasted_iota(jnp.int32, probe_modes.shape, 0) == core
    probe_modes = widen(jnp.where(own, plane[None], swapped[None]), 128.0)
    return (object_field, probe_modes)


def solution(mesh):
    return jax.shard_map(
        on_device,
        mesh=mesh,
        in_specs=(
            P(None, "region", "scan"),
            P(),
            P("region", "scan", None, None, None),
            P("region", "scan", None),
            P("region", "scan", None),
            P(),
            P(),
        ),
        out_specs=(P(None, "region", "scan"), P()),
        check_vma=False,
    )
```

```python
import math

import jax
import jax.numpy as jnp
import ml_dtypes
import numpy as np
from jax import lax
from jax.experimental import pallas as pl
from jax.experimental.pallas import tpu as pltpu
from jax.sharding import PartitionSpec as P


UNROLL = 8
GRANT = 42


def padded_2(cells, sides, width):
    for axis, dim in sides:
        count = lax.axis_size(axis)
        ends = count - 1
        head = lax.slice_in_dim(cells, 0, width, axis=dim)
        tail = lax.slice_in_dim(cells, cells.shape[dim] - width, cells.shape[dim], axis=dim)
        cells = jnp.concatenate(
            [
                lax.ppermute(tail, axis, [(i, (i + 1) % count) for i in range(ends)]),
                cells,
                lax.ppermute(head, axis, [((i + 1) % count, i) for i in range(ends)]),
            ],
            axis=dim,
        )
    return cells


def fourier_tables(length):
    position = np.arange(length)
    angles = (position[:, None] * position[None, :] % length) * (2.0 * math.pi / length)
    table_scale = 1.0 / math.sqrt(length)
    cosine_table = (np.cos(angles) * table_scale).astype(ml_dtypes.bfloat16)
    sine_table = (np.sin(angles) * table_scale).astype(ml_dtypes.bfloat16)
    order = mirrored(length)
    half = length // 2
    folded = np.concatenate(
        [cosine_table[:half], cosine_table[half : half + 1], sine_table[1:half]], axis=0
    )
    cosine_table, sine_table = cosine_table[:, order], sine_table[:, order]
    tables = (folded, folded.T, cosine_table, sine_table, cosine_table.T, sine_table.T)
    return jnp.asarray(np.stack(tables))


def mirrored(length):
    half = length // 2
    return np.concatenate([np.arange(half + 1), np.arange(length - 1, half, -1)])


def combined(even, odd, swapped_even, swapped_odd, edge):
    return (
        even + jnp.where(edge, 0.0, odd),
        jnp.where(edge, swapped_odd, even) - jnp.where(edge, 0.0, odd),
        swapped_even - jnp.where(edge, 0.0, swapped_odd),
        jnp.where(edge, odd, swapped_even) + jnp.where(edge, 0.0, swapped_odd),
    )


def folded_pass(waves, folded, folded_across):
    length = folded.shape[0]
    half = length // 2
    slots = len(waves)
    wide = jnp.concatenate([part.astype(jnp.bfloat16) for pair in waves for part in pair], axis=1)
    first = jnp.dot(folded, wide, preferred_element_type=jnp.float32)
    edge = lax.broadcasted_iota(jnp.int32, (half, length), 0) == 0
    middle = []
    for slot in range(slots):
        real = first[:, 2 * slot * length : (2 * slot + 1) * length]
        imag = first[:, (2 * slot + 1) * length : (2 * slot + 2) * length]
        parts = combined(real[:half], imag[half:], imag[:half], real[half:], edge)
        middle += [part.astype(jnp.bfloat16) for part in parts]
    middle = jnp.concatenate(middle, axis=0)
    second = jnp.dot(middle, folded_across, preferred_element_type=jnp.float32)
    edge = lax.broadcasted_iota(jnp.int32, (length, half), 1) == 0
    out = []
    for slot in range(slots):
        real = second[2 * slot * length : (2 * slot + 1) * length]
        imag = second[(2 * slot + 1) * length : (2 * slot + 2) * length]
        parts = combined(real[:, :half], imag[:, half:], imag[:, :half], real[:, half:], edge)
        out.append(jnp.concatenate(parts, axis=1))
    return jnp.concatenate(out, axis=0)


def fourier_pass(wide, left, right):
    length = wide.shape[0] // 2
    middle = jnp.dot(left, wide, preferred_element_type=jnp.float32).astype(jnp.bfloat16)
    middle = jnp.concatenate(
        [
            jnp.concatenate([middle[:length, cut], middle[length:, cut]], axis=1)
            for cut in (slice(i, i + length) for i in range(0, wide.shape[1], length))
        ],
        axis=0,
    )
    return jnp.dot(middle, right, preferred_element_type=jnp.float32)


def stacked(pairs):
    return jnp.concatenate(
        [jnp.concatenate(pair, axis=0).astype(jnp.bfloat16) for pair in pairs], axis=1
    )


def gradients_kernel(
    place_ref,
    block_hbm,
    above_hbm,
    below_hbm,
    left_hbm,
    right_hbm,
    probe_hbm,
    pattern_hbm,
    tables_hbm,
    rim_left_ref,
    center_ref,
    rim_right_ref,
    mine_ref,
    other_ref,
    block_ref,
    above_ref,
    below_ref,
    left_ref,
    right_ref,
    probe_ref,
    pattern_ref,
    tables_ref,
    left_table_ref,
    right_table_ref,
    padded_ref,
    window_ref,
    far_ref,
    level_ref,
    object_ref,
    probe_sem,
    piece_sem,
):
    modes, length = probe_ref.shape[1], probe_ref.shape[2]
    half = length // 2
    rows, cols = block_ref.shape[1], block_ref.shape[2]
    wide = padded_ref.shape[2]
    slots = pattern_ref.shape[0]

    def fetch_probe(mode):
        return pltpu.make_async_copy(
            probe_hbm.at[:, mode], probe_ref.at[:, mode], probe_sem.at[mode]
        )

    fetches = [
        pltpu.make_async_copy(source, target, piece_sem.at[index])
        for index, (source, target) in enumerate(
            (
                (left_hbm, left_ref),
                (right_hbm, right_ref),
                (above_hbm, above_ref),
                (below_hbm, below_ref),
                (block_hbm, block_ref),
                (tables_hbm, tables_ref),
                (pattern_hbm, pattern_ref),
            )
        )
    ]
    for fetch in fetches[5:6] + fetches[:5] + fetches[6:]:
        fetch.start()
    for mode in range(modes):
        fetch_probe(mode).start()
    for part_ref in (rim_left_ref, center_ref, rim_right_ref, level_ref, object_ref):
        part_ref[...] = jnp.zeros_like(part_ref)
    fetches[5].wait()
    low, high = slice(0, length), slice(length, 2 * length)
    for table_ref, cosine, sine in (
        (left_table_ref, tables_ref[2], -tables_ref[3]),
        (right_table_ref, tables_ref[4], tables_ref[5]),
    ):
        table_ref[low, low] = cosine
        table_ref[high, high] = cosine
        table_ref[low, high] = sine
        table_ref[high, low] = -sine
    for fetch in fetches[:5]:
        fetch.wait()
    padded_ref[:, :, :half] = left_ref[...].astype(jnp.float32)
    padded_ref[:, :, half + cols :] = right_ref[...].astype(jnp.float32)
    padded_ref[:, :half, half : half + cols] = above_ref[...].astype(jnp.float32)
    padded_ref[:, half + rows :, half : half + cols] = below_ref[...].astype(jnp.float32)
    padded_ref[:, half : half + rows, half : half + cols] = (
        block_ref[...].astype(jnp.bfloat16).astype(jnp.float32)
    )
    first = place_ref[2, 0] == 0
    places = []
    for slot in range(slots):
        row, col = place_ref[0, slot], place_ref[1, slot]
        shift = row % 8
        span = pl.ds(pl.multiple_of(row - shift, 8), length + 8)
        places.append((span, shift, col))
        for part in range(2):
            strip = pltpu.roll(padded_ref[part, span, :], wide - col, 1)[:, :length]
            window_ref[slot, part] = pltpu.roll(strip, length + 8 - shift, 0)[:length]
    fetches[6].wait()

    def go_forward(mode, carry):
        fetch_probe(mode).wait()
        probe_real, probe_imag = probe_ref[0, mode], probe_ref[1, mode]
        waves = []
        for slot in range(slots):
            win_real, win_imag = window_ref[slot, 0], window_ref[slot, 1]
            waves.append(
                (
                    probe_real * win_real - probe_imag * win_imag,
                    probe_real * win_imag + probe_imag * win_real,
                )
            )
        far = folded_pass(waves, tables_ref[0], tables_ref[1])
        far_ref[mode] = far
        far_real, far_imag = far[:, :length], far[:, length:]
        level_ref[...] += far_real * far_real + far_imag * far_imag
        return carry

    lax.fori_loop(0, modes, go_forward, 0, unroll=UNROLL)
    amplitude = jnp.maximum(jnp.sqrt(level_ref[...]), 1.0)
    targets = jnp.concatenate([pattern_ref[slot] for slot in range(slots)], axis=0)
    level_ref[...] = 1.0 - jnp.sqrt(targets) / amplitude

    def go_back(mode, carry):
        corrected = []
        for slot in range(slots):
            band = slice(slot * length, (slot + 1) * length)
            factor = level_ref[band]
            far = far_ref[mode, band]
            corrected.append((factor * far[:, :length], factor * far[:, length:]))
        back = fourier_pass(stacked(corrected), left_table_ref[...], right_table_ref[...])
        probe_real, probe_imag = probe_ref[0, mode], probe_ref[1, mode]
        term_real = term_imag = 0.0
        for slot in range(slots):
            band = slice(slot * length, (slot + 1) * length)
            back_real, back_imag = back[band, :length], back[band, length:]
            object_ref[slot, 0] += probe_real * back_real + probe_imag * back_imag
            object_ref[slot, 1] += probe_real * back_imag - probe_imag * back_real
            win_real, win_imag = window_ref[slot, 0], window_ref[slot, 1]
            term_real += win_real * back_real + win_imag * back_imag
            term_imag += win_real * back_imag - win_imag * back_real
        mine_ref[mode] = jnp.where(first, term_real, term_imag)
        other_ref[mode] = jnp.where(first, term_imag, term_real)
        return carry

    lax.fori_loop(0, modes, go_back, 0, unroll=UNROLL)
    for slot in range(slots):
        span, shift, col = places[slot]
        for part in range(2):
            strip = jnp.concatenate(
                [object_ref[slot, part], jnp.zeros((8, length), jnp.float32)], axis=0
            )
            strip = pltpu.roll(strip, shift, 0)
            strip = jnp.concatenate(
                [strip, jnp.zeros((length + 8, wide - length), jnp.float32)], axis=1
            )
            strip = pltpu.roll(strip, col, 1)
            rim_left_ref[part, span, :] += strip[:, :half]
            center_ref[part, span, :] += strip[:, half : half + cols]
            rim_right_ref[part, span, :] += strip[:, half + cols :]


def device_gradients(place, block, above, below, left, right, probe, pattern):
    tables = fourier_tables(probe.shape[-1])
    _, modes, length, _ = probe.shape
    rows, cols = block.shape[1] + length, block.shape[2] + length
    slots = pattern.shape[0]
    anywhere = pl.BlockSpec(memory_space=pl.ANY)
    f32 = jnp.float32
    fetched = (block, above, below, left, right, probe, pattern, tables)
    made = (
        jax.ShapeDtypeStruct((2, rows, length // 2), f32),
        jax.ShapeDtypeStruct((2, rows, block.shape[2]), f32),
        jax.ShapeDtypeStruct((2, rows, length // 2), f32),
        jax.ShapeDtypeStruct((modes, length, length), f32),
        jax.ShapeDtypeStruct((modes, length, length), f32),
    )
    return pl.pallas_call(
        gradients_kernel,
        out_shape=made,
        in_specs=[pl.BlockSpec(memory_space=pltpu.SMEM)] + [anywhere] * len(fetched),
        out_specs=(pl.BlockSpec(memory_space=pltpu.VMEM),) * len(made),
        scratch_shapes=[pltpu.VMEM(item.shape, item.dtype) for item in fetched]
        + [
            pltpu.VMEM((2 * length, 2 * length), jnp.bfloat16),
            pltpu.VMEM((2 * length, 2 * length), jnp.bfloat16),
            pltpu.VMEM((2, rows, cols), f32),
            pltpu.VMEM((slots, 2, length, length), f32),
            pltpu.VMEM((modes, slots * length, 2 * length), f32),
            pltpu.VMEM((slots * length, length), f32),
            pltpu.VMEM((slots, 2, length, length), f32),
            pltpu.SemaphoreType.DMA((modes,)),
            pltpu.SemaphoreType.DMA((8,)),
        ],
        compiler_params=pltpu.CompilerParams(vmem_limit_bytes=GRANT * 1024 * 1024),
        cost_estimate=pl.CostEstimate(
            flops=slots * modes * 32 * length**3, bytes_accessed=16 * 2**20, transcendentals=0
        ),
    )(place, *fetched)


def axis_groups(kept):
    rows, cols = lax.axis_size("region"), lax.axis_size("scan")
    sizes = {"core": 2, "x": cols // 2, "y": 4, "pair": 2, "far": rows // 8}
    groups = {}
    for device in range(rows * cols):
        place, rest = {}, device
        for name in sizes:
            place[name] = rest % sizes[name]
            rest = rest // sizes[name]
        key = tuple(place[name] for name in place if name not in kept)
        groups.setdefault(key, []).append(device)
    return [groups[key] for key in sorted(groups)]


def narrow(values, scale):
    return (values * (1.0 / scale)).astype(jnp.float16)


def widen(values, scale):
    return values.astype(jnp.float32) * scale


def exchange(parts, kept):
    return lax.all_to_all(parts, ("region", "scan"), 0, 0, axis_index_groups=axis_groups(kept))


def swap_cores(values):
    count = lax.axis_size("region") * lax.axis_size("scan")
    return lax.ppermute(values, ("region", "scan"), [(i, i ^ 1) for i in range(count)])


def shift_far(values, step):
    cols = lax.axis_size("scan")
    count = lax.axis_size("region") * cols
    stride = 8 * cols
    pairs = [(i, (i + step * stride) % count) for i in range(count)]
    return lax.ppermute(values, ("region", "scan"), pairs)


def sum_scattered(mine, other):
    modes, rows, cols = mine.shape
    pair = mine + widen(swap_cores(narrow(other, 8.0)), 8.0)
    places = 8 * (lax.axis_size("scan") // 2)
    pieces = narrow(pair, 16.0).reshape(places, modes * rows // places, cols)
    pieces = exchange(pieces, ("pair", "y", "x"))
    return jnp.sum(widen(pieces, 16.0), axis=0)


def sum_far(piece):
    sent = narrow(piece, 512.0)
    one, two, three = (widen(shift_far(sent, step), 512.0) for step in (1, 2, 3))
    return (widen(sent, 512.0) + two) + (one + three)


def gather_all(total, modes):
    rows, cols = total.shape
    places = 8 * (lax.axis_size("scan") // 2)
    pieces = jnp.broadcast_to(total, (places, rows, cols))
    return exchange(pieces, ("pair", "y", "x")).reshape(modes, -1, cols)


def neighbours(head, tail, axis):
    count = lax.axis_size(axis)
    even = lax.axis_index(axis) % 2 == 0
    swaps = [
        [pair for i in range(start, count - 1, 2) for pair in ((i, i + 1), (i + 1, i))]
        for start in (0, 1)
    ]
    inner = lax.ppermute(jnp.where(even, tail, head), axis, swaps[0])
    outer = lax.ppermute(jnp.where(even, head, tail), axis, swaps[1])
    return (jnp.where(even, outer, inner), jnp.where(even, inner, outer))


def edges(cells, axis, dim, width):
    head = lax.slice_in_dim(cells, 0, width, axis=dim)
    tail = lax.slice_in_dim(cells, cells.shape[dim] - width, cells.shape[dim], axis=dim)
    return neighbours(head, tail, axis)


def trade(head, tail, axis):
    return neighbours(narrow(head, 64.0), narrow(tail, 64.0), axis)


def on_device(object_field, probe_modes, pattern, rows_at, cols_at, object_step, probe_step):
    half_width = probe_modes.shape[-1] // 2
    block_rows = object_field.shape[1]
    block_cols = object_field.shape[2]
    core = lax.axis_index("scan") % 2
    place = jnp.stack(
        [
            rows_at[0, 0] % block_rows,
            cols_at[0, 0] % block_cols,
            jnp.broadcast_to(core, rows_at.shape[2:]).astype(jnp.int32),
        ]
    )
    targets = pattern[0, 0]
    for dim in (1, 2):
        nearer = lax.slice_in_dim(targets, 0, half_width + 1, axis=dim)
        farther = lax.slice_in_dim(targets, half_width + 1, 2 * half_width, axis=dim)
        targets = jnp.concatenate([nearer, lax.rev(farther, (dim,))], axis=dim)
    cells = object_field.astype(jnp.bfloat16)
    above, below = edges(cells, "region", 1, half_width)
    tall = jnp.concatenate([above, cells, below], axis=1)
    left, right = edges(tall, "scan", 2, half_width)
    rim_left, center, rim_right, mine, other = device_gradients(
        place, object_field, above, below, left, right, probe_modes, targets
    )
    piece = sum_scattered(mine, other)
    from_left, from_right = trade(rim_left, rim_right, "scan")
    center = center + widen(jnp.concatenate([from_left, from_right], axis=2), 64.0)
    region, scan = lax.axis_index("region"), lax.axis_index("scan")
    spot = (region % 8 * 4 + scan // 2) * piece.shape[0]
    flat = probe_modes.reshape(2, -1, probe_modes.shape[-1])
    mine = lax.dynamic_slice(flat, (core, spot, 0), (1, *piece.shape))[0]
    piece, mine = lax.optimization_barrier((piece, mine))
    total = sum_far(piece)
    updated = narrow(mine - probe_step[0] * total, 128.0)
    updated, center = lax.optimization_barrier((updated, center))
    from_above, from_below = trade(center[:, :half_width], center[:, -half_width:], "region")
    plane = gather_all(updated, probe_modes.shape[1])
    plane, from_above, from_below = lax.optimization_barrier((plane, from_above, from_below))
    swapped = swap_cores(plane)
    inner = center[:, half_width:-half_width]
    inner = inner + widen(jnp.concatenate([from_above, from_below], axis=1), 64.0)
    object_field = object_field - object_step[0] * inner
    own = lax.broadcasted_iota(jnp.int32, probe_modes.shape, 0) == core
    probe_modes = widen(jnp.where(own, plane[None], swapped[None]), 128.0)
    return (object_field, probe_modes)


def solution(mesh):
    return jax.shard_map(
        on_device,
        mesh=mesh,
        in_specs=(
            P(None, "region", "scan"),
            P(),
            P("region", "scan", None, None, None),
            P("region", "scan", None),
            P("region", "scan", None),
            P(),
            P(),
        ),
        out_specs=(P(None, "region", "scan"), P()),
        check_vma=False,
    )
```

```python
import math

import jax
import jax.numpy as jnp
import ml_dtypes
import numpy as np
from jax import lax
from jax.experimental import pallas as pl
from jax.experimental.pallas import tpu as pltpu
from jax.sharding import PartitionSpec as P


UNROLL = 8
GRANT = 42


def padded_2(cells, sides, width):
    for axis, dim in sides:
        count = lax.axis_size(axis)
        ends = count - 1
        head = lax.slice_in_dim(cells, 0, width, axis=dim)
        tail = lax.slice_in_dim(cells, cells.shape[dim] - width, cells.shape[dim], axis=dim)
        cells = jnp.concatenate(
            [
                lax.ppermute(tail, axis, [(i, (i + 1) % count) for i in range(ends)]),
                cells,
                lax.ppermute(head, axis, [((i + 1) % count, i) for i in range(ends)]),
            ],
            axis=dim,
        )
    return cells


def fourier_tables(length):
    position = np.arange(length)
    angles = (position[:, None] * position[None, :] % length) * (2.0 * math.pi / length)
    table_scale = 1.0 / math.sqrt(length)
    cosine_table = (np.cos(angles) * table_scale).astype(ml_dtypes.bfloat16)
    sine_table = (np.sin(angles) * table_scale).astype(ml_dtypes.bfloat16)
    order = mirrored(length)
    half = length // 2
    folded = np.concatenate(
        [cosine_table[:half], cosine_table[half : half + 1], sine_table[1:half]], axis=0
    )
    cosine_table, sine_table = cosine_table[:, order], sine_table[:, order]
    tables = (folded, folded.T, cosine_table, sine_table, cosine_table.T, sine_table.T)
    return jnp.asarray(np.stack(tables))


def mirrored(length):
    half = length // 2
    return np.concatenate([np.arange(half + 1), np.arange(length - 1, half, -1)])


def combined(even, odd, swapped_even, swapped_odd, edge):
    return (
        even + jnp.where(edge, 0.0, odd),
        jnp.where(edge, swapped_odd, even) - jnp.where(edge, 0.0, odd),
        swapped_even - jnp.where(edge, 0.0, swapped_odd),
        jnp.where(edge, odd, swapped_even) + jnp.where(edge, 0.0, swapped_odd),
    )


def folded_pass(waves, folded, folded_across):
    length = folded.shape[0]
    half = length // 2
    slots = len(waves)
    wide = jnp.concatenate([part.astype(jnp.bfloat16) for pair in waves for part in pair], axis=1)
    first = jnp.dot(folded, wide, preferred_element_type=jnp.float32)
    edge = lax.broadcasted_iota(jnp.int32, (half, length), 0) == 0
    middle = []
    for slot in range(slots):
        real = first[:, 2 * slot * length : (2 * slot + 1) * length]
        imag = first[:, (2 * slot + 1) * length : (2 * slot + 2) * length]
        parts = combined(real[:half], imag[half:], imag[:half], real[half:], edge)
        middle += [part.astype(jnp.bfloat16) for part in parts]
    middle = jnp.concatenate(middle, axis=0)
    second = jnp.dot(middle, folded_across, preferred_element_type=jnp.float32)
    edge = lax.broadcasted_iota(jnp.int32, (length, half), 1) == 0
    out = []
    for slot in range(slots):
        real = second[2 * slot * length : (2 * slot + 1) * length]
        imag = second[(2 * slot + 1) * length : (2 * slot + 2) * length]
        parts = combined(real[:, :half], imag[:, half:], imag[:, :half], real[:, half:], edge)
        out.append(jnp.concatenate(parts, axis=1))
    return jnp.concatenate(out, axis=0)


def fourier_pass(wide, left, right):
    length = wide.shape[0] // 2
    middle = jnp.dot(left, wide, preferred_element_type=jnp.float32).astype(jnp.bfloat16)
    middle = jnp.concatenate(
        [
            jnp.concatenate([middle[:length, cut], middle[length:, cut]], axis=1)
            for cut in (slice(i, i + length) for i in range(0, wide.shape[1], length))
        ],
        axis=0,
    )
    return jnp.dot(middle, right, preferred_element_type=jnp.float32)


def stacked(pairs):
    return jnp.concatenate(
        [jnp.concatenate(pair, axis=0).astype(jnp.bfloat16) for pair in pairs], axis=1
    )


def gradients_kernel(
    place_ref,
    block_hbm,
    above_hbm,
    below_hbm,
    left_hbm,
    right_hbm,
    probe_hbm,
    pattern_hbm,
    tables_hbm,
    rim_left_ref,
    center_ref,
    rim_right_ref,
    mine_ref,
    other_ref,
    block_ref,
    above_ref,
    below_ref,
    left_ref,
    right_ref,
    probe_ref,
    pattern_ref,
    tables_ref,
    left_table_ref,
    right_table_ref,
    padded_ref,
    window_ref,
    far_ref,
    level_ref,
    object_ref,
    probe_sem,
    piece_sem,
):
    modes, length = probe_ref.shape[1], probe_ref.shape[2]
    half = length // 2
    rows, cols = block_ref.shape[1], block_ref.shape[2]
    wide = padded_ref.shape[2]
    slots = pattern_ref.shape[0]

    def fetch_probe(mode):
        return pltpu.make_async_copy(
            probe_hbm.at[:, mode], probe_ref.at[:, mode], probe_sem.at[mode]
        )

    fetches = [
        pltpu.make_async_copy(source, target, piece_sem.at[index])
        for index, (source, target) in enumerate(
            (
                (left_hbm, left_ref),
                (right_hbm, right_ref),
                (above_hbm, above_ref),
                (below_hbm, below_ref),
                (block_hbm, block_ref),
                (tables_hbm, tables_ref),
                (pattern_hbm, pattern_ref),
            )
        )
    ]
    for fetch in fetches[5:6] + fetches[:5] + fetches[6:]:
        fetch.start()
    for mode in range(modes):
        fetch_probe(mode).start()
    for part_ref in (rim_left_ref, center_ref, rim_right_ref, level_ref, object_ref):
        part_ref[...] = jnp.zeros_like(part_ref)
    fetches[5].wait()
    low, high = slice(0, length), slice(length, 2 * length)
    for table_ref, cosine, sine in (
        (left_table_ref, tables_ref[2], -tables_ref[3]),
        (right_table_ref, tables_ref[4], tables_ref[5]),
    ):
        table_ref[low, low] = cosine
        table_ref[high, high] = cosine
        table_ref[low, high] = sine
        table_ref[high, low] = -sine
    for fetch in fetches[:5]:
        fetch.wait()
    padded_ref[:, :, :half] = left_ref[...].astype(jnp.float32)
    padded_ref[:, :, half + cols :] = right_ref[...].astype(jnp.float32)
    padded_ref[:, :half, half : half + cols] = above_ref[...].astype(jnp.float32)
    padded_ref[:, half + rows :, half : half + cols] = below_ref[...].astype(jnp.float32)
    padded_ref[:, half : half + rows, half : half + cols] = (
        block_ref[...].astype(jnp.bfloat16).astype(jnp.float32)
    )
    first = place_ref[2, 0] == 0
    places = []
    for slot in range(slots):
        row, col = place_ref[0, slot], place_ref[1, slot]
        shift = row % 8
        span = pl.ds(pl.multiple_of(row - shift, 8), length + 8)
        places.append((span, shift, col))
        for part in range(2):
            strip = pltpu.roll(padded_ref[part, span, :], wide - col, 1)[:, :length]
            window_ref[slot, part] = pltpu.roll(strip, length + 8 - shift, 0)[:length]
    fetches[6].wait()

    def go_forward(mode, carry):
        fetch_probe(mode).wait()
        probe_real, probe_imag = probe_ref[0, mode], probe_ref[1, mode]
        waves = []
        for slot in range(slots):
            win_real, win_imag = window_ref[slot, 0], window_ref[slot, 1]
            waves.append(
                (
                    probe_real * win_real - probe_imag * win_imag,
                    probe_real * win_imag + probe_imag * win_real,
                )
            )
        far = folded_pass(waves, tables_ref[0], tables_ref[1])
        far_ref[mode] = far
        far_real, far_imag = far[:, :length], far[:, length:]
        level_ref[...] += far_real * far_real + far_imag * far_imag
        return carry

    lax.fori_loop(0, modes, go_forward, 0, unroll=UNROLL)
    amplitude = jnp.maximum(jnp.sqrt(level_ref[...]), 1.0)
    targets = jnp.concatenate([pattern_ref[slot] for slot in range(slots)], axis=0)
    level_ref[...] = 1.0 - targets / amplitude

    def go_back(mode, carry):
        corrected = []
        for slot in range(slots):
            band = slice(slot * length, (slot + 1) * length)
            factor = level_ref[band]
            far = far_ref[mode, band]
            corrected.append((factor * far[:, :length], factor * far[:, length:]))
        back = fourier_pass(stacked(corrected), left_table_ref[...], right_table_ref[...])
        probe_real, probe_imag = probe_ref[0, mode], probe_ref[1, mode]
        term_real = term_imag = 0.0
        for slot in range(slots):
            band = slice(slot * length, (slot + 1) * length)
            back_real, back_imag = back[band, :length], back[band, length:]
            object_ref[slot, 0] += probe_real * back_real + probe_imag * back_imag
            object_ref[slot, 1] += probe_real * back_imag - probe_imag * back_real
            win_real, win_imag = window_ref[slot, 0], window_ref[slot, 1]
            term_real += win_real * back_real + win_imag * back_imag
            term_imag += win_real * back_imag - win_imag * back_real
        mine_ref[mode] = jnp.where(first, term_real, term_imag)
        other_ref[mode] = jnp.where(first, term_imag, term_real)
        return carry

    lax.fori_loop(0, modes, go_back, 0, unroll=UNROLL)
    for slot in range(slots):
        span, shift, col = places[slot]
        for part in range(2):
            strip = jnp.concatenate(
                [object_ref[slot, part], jnp.zeros((8, length), jnp.float32)], axis=0
            )
            strip = pltpu.roll(strip, shift, 0)
            strip = jnp.concatenate(
                [strip, jnp.zeros((length + 8, wide - length), jnp.float32)], axis=1
            )
            strip = pltpu.roll(strip, col, 1)
            rim_left_ref[part, span, :] += strip[:, :half]
            center_ref[part, span, :] += strip[:, half : half + cols]
            rim_right_ref[part, span, :] += strip[:, half + cols :]


def device_gradients(place, block, above, below, left, right, probe, pattern):
    tables = fourier_tables(probe.shape[-1])
    _, modes, length, _ = probe.shape
    rows, cols = block.shape[1] + length, block.shape[2] + length
    slots = pattern.shape[0]
    anywhere = pl.BlockSpec(memory_space=pl.ANY)
    f32 = jnp.float32
    fetched = (block, above, below, left, right, probe, pattern, tables)
    made = (
        jax.ShapeDtypeStruct((2, rows, length // 2), f32),
        jax.ShapeDtypeStruct((2, rows, block.shape[2]), f32),
        jax.ShapeDtypeStruct((2, rows, length // 2), f32),
        jax.ShapeDtypeStruct((modes, length, length), f32),
        jax.ShapeDtypeStruct((modes, length, length), f32),
    )
    return pl.pallas_call(
        gradients_kernel,
        out_shape=made,
        in_specs=[pl.BlockSpec(memory_space=pltpu.SMEM)] + [anywhere] * len(fetched),
        out_specs=(pl.BlockSpec(memory_space=pltpu.VMEM),) * len(made),
        scratch_shapes=[pltpu.VMEM(item.shape, item.dtype) for item in fetched]
        + [
            pltpu.VMEM((2 * length, 2 * length), jnp.bfloat16),
            pltpu.VMEM((2 * length, 2 * length), jnp.bfloat16),
            pltpu.VMEM((2, rows, cols), f32),
            pltpu.VMEM((slots, 2, length, length), f32),
            pltpu.VMEM((modes, slots * length, 2 * length), f32),
            pltpu.VMEM((slots * length, length), f32),
            pltpu.VMEM((slots, 2, length, length), f32),
            pltpu.SemaphoreType.DMA((modes,)),
            pltpu.SemaphoreType.DMA((8,)),
        ],
        compiler_params=pltpu.CompilerParams(vmem_limit_bytes=GRANT * 1024 * 1024),
        cost_estimate=pl.CostEstimate(
            flops=slots * modes * 32 * length**3, bytes_accessed=16 * 2**20, transcendentals=0
        ),
    )(place, *fetched)


def axis_groups(kept):
    rows, cols = lax.axis_size("region"), lax.axis_size("scan")
    sizes = {"core": 2, "x": cols // 2, "y": 4, "pair": 2, "far": rows // 8}
    groups = {}
    for device in range(rows * cols):
        place, rest = {}, device
        for name in sizes:
            place[name] = rest % sizes[name]
            rest = rest // sizes[name]
        key = tuple(place[name] for name in place if name not in kept)
        groups.setdefault(key, []).append(device)
    return [groups[key] for key in sorted(groups)]


def narrow(values, scale):
    return (values * (1.0 / scale)).astype(jnp.float16)


def widen(values, scale):
    return values.astype(jnp.float32) * scale


def exchange(parts, kept):
    return lax.all_to_all(parts, ("region", "scan"), 0, 0, axis_index_groups=axis_groups(kept))


def swap_cores(values):
    count = lax.axis_size("region") * lax.axis_size("scan")
    return lax.ppermute(values, ("region", "scan"), [(i, i ^ 1) for i in range(count)])


def shift_far(values, step):
    cols = lax.axis_size("scan")
    count = lax.axis_size("region") * cols
    stride = 8 * cols
    pairs = [(i, (i + step * stride) % count) for i in range(count)]
    return lax.ppermute(values, ("region", "scan"), pairs)


def sum_scattered(mine, other):
    modes, rows, cols = mine.shape
    pair = mine + widen(swap_cores(narrow(other, 8.0)), 8.0)
    places = 8 * (lax.axis_size("scan") // 2)
    pieces = narrow(pair, 16.0).reshape(places, modes * rows // places, cols)
    pieces = exchange(pieces, ("pair", "y", "x"))
    return jnp.sum(widen(pieces, 16.0), axis=0)


def sum_far(piece):
    sent = narrow(piece, 512.0)
    one, two, three = (widen(shift_far(sent, step), 512.0) for step in (1, 2, 3))
    return (widen(sent, 512.0) + two) + (one + three)


def gather_all(total, modes):
    rows, cols = total.shape
    places = 8 * (lax.axis_size("scan") // 2)
    pieces = jnp.broadcast_to(total, (places, rows, cols))
    return exchange(pieces, ("pair", "y", "x")).reshape(modes, -1, cols)


def neighbours(head, tail, axis, kind):
    count = lax.axis_size(axis)
    even = lax.axis_index(axis) % 2 == 0
    swaps = [
        [pair for i in range(start, count - 1, 2) for pair in ((i, i + 1), (i + 1, i))]
        for start in (0, 1)
    ]
    outer = lax.ppermute(jnp.where(even, head, tail).astype(kind), axis, swaps[1])
    inner = lax.ppermute(jnp.where(even, tail, head).astype(kind), axis, swaps[0])
    return (jnp.where(even, outer, inner), jnp.where(even, inner, outer))


def trade(head, tail, axis):
    return neighbours(narrow(head, 64.0), narrow(tail, 64.0), axis, jnp.float16)


def on_device(object_field, probe_modes, pattern, rows_at, cols_at, object_step, probe_step):
    half_width = probe_modes.shape[-1] // 2
    block_rows = object_field.shape[1]
    block_cols = object_field.shape[2]
    core = lax.axis_index("scan") % 2
    place = jnp.stack(
        [
            rows_at[0, 0] % block_rows,
            cols_at[0, 0] % block_cols,
            jnp.broadcast_to(core, rows_at.shape[2:]).astype(jnp.int32),
        ]
    )
    targets = jnp.sqrt(pattern[0, 0])
    for dim in (1, 2):
        nearer = lax.slice_in_dim(targets, 0, half_width + 1, axis=dim)
        farther = lax.slice_in_dim(targets, half_width + 1, 2 * half_width, axis=dim)
        targets = jnp.concatenate([nearer, lax.rev(farther, (dim,))], axis=dim)
    kind = jnp.bfloat16
    above, below = neighbours(
        object_field[:, :half_width], object_field[:, -half_width:], "region", kind
    )
    sides = [
        jnp.concatenate([above[:, :, cut], object_field[:, :, cut].astype(kind), below[:, :, cut]], 1)
        for cut in (slice(0, half_width), slice(block_cols - half_width, block_cols))
    ]
    left, right = neighbours(*sides, "scan", kind)
    rim_left, center, rim_right, mine, other = device_gradients(
        place, object_field, above, below, left, right, probe_modes, targets
    )
    piece = sum_scattered(mine, other)
    from_left, from_right = trade(rim_left, rim_right, "scan")
    center = center + widen(jnp.concatenate([from_left, from_right], axis=2), 64.0)
    region, scan = lax.axis_index("region"), lax.axis_index("scan")
    spot = (region % 8 * 4 + scan // 2) * piece.shape[0]
    flat = probe_modes.reshape(2, -1, probe_modes.shape[-1])
    mine = lax.dynamic_slice(flat, (core, spot, 0), (1, *piece.shape))[0]
    piece, mine = lax.optimization_barrier((piece, mine))
    total = sum_far(piece)
    updated = narrow(mine - probe_step[0] * total, 128.0)
    updated, center = lax.optimization_barrier((updated, center))
    from_above, from_below = trade(center[:, :half_width], center[:, -half_width:], "region")
    plane = gather_all(updated, probe_modes.shape[1])
    plane, from_above, from_below = lax.optimization_barrier((plane, from_above, from_below))
    swapped = swap_cores(plane)
    inner = center[:, half_width:-half_width]
    inner = inner + widen(jnp.concatenate([from_above, from_below], axis=1), 64.0)
    object_field = object_field - object_step[0] * inner
    own = lax.broadcasted_iota(jnp.int32, probe_modes.shape, 0) == core
    probe_modes = widen(jnp.where(own, plane[None], swapped[None]), 128.0)
    return (object_field, probe_modes)


def solution(mesh):
    return jax.shard_map(
        on_device,
        mesh=mesh,
        in_specs=(
            P(None, "region", "scan"),
            P(),
            P("region", "scan", None, None, None),
            P("region", "scan", None),
            P("region", "scan", None),
            P(),
            P(),
        ),
        out_specs=(P(None, "region", "scan"), P()),
        check_vma=False,
    )
```

```python
import math

import jax
import jax.numpy as jnp
import ml_dtypes
import numpy as np
from jax import lax
from jax.experimental import pallas as pl
from jax.experimental.pallas import tpu as pltpu
from jax.sharding import PartitionSpec as P


UNROLL = 8
GRANT = 42


def padded_2(cells, sides, width):
    for axis, dim in sides:
        count = lax.axis_size(axis)
        ends = count - 1
        head = lax.slice_in_dim(cells, 0, width, axis=dim)
        tail = lax.slice_in_dim(cells, cells.shape[dim] - width, cells.shape[dim], axis=dim)
        cells = jnp.concatenate(
            [
                lax.ppermute(tail, axis, [(i, (i + 1) % count) for i in range(ends)]),
                cells,
                lax.ppermute(head, axis, [((i + 1) % count, i) for i in range(ends)]),
            ],
            axis=dim,
        )
    return cells


def fourier_tables(length):
    position = np.arange(length)
    angles = (position[:, None] * position[None, :] % length) * (2.0 * math.pi / length)
    table_scale = 1.0 / math.sqrt(length)
    cosine_table = (np.cos(angles) * table_scale).astype(ml_dtypes.bfloat16)
    sine_table = (np.sin(angles) * table_scale).astype(ml_dtypes.bfloat16)
    order = mirrored(length)
    half = length // 2
    folded = np.concatenate(
        [cosine_table[:half], cosine_table[half : half + 1], sine_table[1:half]], axis=0
    )
    cosine_table, sine_table = cosine_table[:, order], sine_table[:, order]
    tables = (folded, folded.T, cosine_table, sine_table, cosine_table.T, sine_table.T)
    return jnp.asarray(np.stack(tables))


def mirrored(length):
    half = length // 2
    return np.concatenate([np.arange(half + 1), np.arange(length - 1, half, -1)])


def combined(even, odd, swapped_even, swapped_odd, edge):
    return (
        even + jnp.where(edge, 0.0, odd),
        jnp.where(edge, swapped_odd, even) - jnp.where(edge, 0.0, odd),
        swapped_even - jnp.where(edge, 0.0, swapped_odd),
        jnp.where(edge, odd, swapped_even) + jnp.where(edge, 0.0, swapped_odd),
    )


def folded_pass(waves, folded, folded_across):
    length = folded.shape[0]
    half = length // 2
    slots = len(waves)
    wide = jnp.concatenate([part.astype(jnp.bfloat16) for pair in waves for part in pair], axis=1)
    first = jnp.dot(folded, wide, preferred_element_type=jnp.float32)
    edge = lax.broadcasted_iota(jnp.int32, (half, length), 0) == 0
    middle = []
    for slot in range(slots):
        real = first[:, 2 * slot * length : (2 * slot + 1) * length]
        imag = first[:, (2 * slot + 1) * length : (2 * slot + 2) * length]
        parts = combined(real[:half], imag[half:], imag[:half], real[half:], edge)
        middle += [part.astype(jnp.bfloat16) for part in parts]
    middle = jnp.concatenate(middle, axis=0)
    second = jnp.dot(middle, folded_across, preferred_element_type=jnp.float32)
    edge = lax.broadcasted_iota(jnp.int32, (length, half), 1) == 0
    out = []
    for slot in range(slots):
        real = second[2 * slot * length : (2 * slot + 1) * length]
        imag = second[(2 * slot + 1) * length : (2 * slot + 2) * length]
        parts = combined(real[:, :half], imag[:, half:], imag[:, :half], real[:, half:], edge)
        out.append(jnp.concatenate(parts, axis=1))
    return jnp.concatenate(out, axis=0)


def fourier_pass(wide, left, right):
    length = wide.shape[0] // 2
    middle = jnp.dot(left, wide, preferred_element_type=jnp.float32).astype(jnp.bfloat16)
    middle = jnp.concatenate(
        [
            jnp.concatenate([middle[:length, cut], middle[length:, cut]], axis=1)
            for cut in (slice(i, i + length) for i in range(0, wide.shape[1], length))
        ],
        axis=0,
    )
    return jnp.dot(middle, right, preferred_element_type=jnp.float32)


def stacked(pairs):
    return jnp.concatenate(
        [jnp.concatenate(pair, axis=0).astype(jnp.bfloat16) for pair in pairs], axis=1
    )


def gradients_kernel(
    place_ref,
    block_hbm,
    above_hbm,
    below_hbm,
    left_hbm,
    right_hbm,
    probe_hbm,
    pattern_hbm,
    tables_hbm,
    rim_left_ref,
    center_ref,
    rim_right_ref,
    mine_ref,
    other_ref,
    block_ref,
    above_ref,
    below_ref,
    left_ref,
    right_ref,
    probe_ref,
    pattern_ref,
    tables_ref,
    left_table_ref,
    right_table_ref,
    padded_ref,
    window_ref,
    far_ref,
    level_ref,
    object_ref,
    probe_sem,
    piece_sem,
):
    modes, length = probe_ref.shape[1], probe_ref.shape[2]
    half = length // 2
    rows, cols = block_ref.shape[1], block_ref.shape[2]
    wide = padded_ref.shape[2]
    slots = pattern_ref.shape[0]

    def fetch_probe(mode):
        return pltpu.make_async_copy(
            probe_hbm.at[:, mode], probe_ref.at[:, mode], probe_sem.at[mode]
        )

    fetches = [
        pltpu.make_async_copy(source, target, piece_sem.at[index])
        for index, (source, target) in enumerate(
            (
                (left_hbm, left_ref),
                (right_hbm, right_ref),
                (above_hbm, above_ref),
                (below_hbm, below_ref),
                (block_hbm, block_ref),
                (tables_hbm, tables_ref),
                (pattern_hbm, pattern_ref),
            )
        )
    ]
    for fetch in fetches:
        fetch.start()
    for mode in range(modes):
        fetch_probe(mode).start()
    for part_ref in (rim_left_ref, center_ref, rim_right_ref, level_ref, object_ref):
        part_ref[...] = jnp.zeros_like(part_ref)
    for fetch in fetches[:5]:
        fetch.wait()
    padded_ref[:, :, :half] = left_ref[...].astype(jnp.float32)
    padded_ref[:, :, half + cols :] = right_ref[...].astype(jnp.float32)
    padded_ref[:, :half, half : half + cols] = above_ref[...].astype(jnp.float32)
    padded_ref[:, half + rows :, half : half + cols] = below_ref[...].astype(jnp.float32)
    padded_ref[:, half : half + rows, half : half + cols] = (
        block_ref[...].astype(jnp.bfloat16).astype(jnp.float32)
    )
    first = place_ref[2, 0] == 0
    places = []
    for slot in range(slots):
        row, col = place_ref[0, slot], place_ref[1, slot]
        shift = row % 8
        span = pl.ds(pl.multiple_of(row - shift, 8), length + 8)
        places.append((span, shift, col))
        for part in range(2):
            strip = pltpu.roll(padded_ref[part, span, :], wide - col, 1)[:, :length]
            window_ref[slot, part] = pltpu.roll(strip, length + 8 - shift, 0)[:length]
    fetches[5].wait()
    low, high = slice(0, length), slice(length, 2 * length)
    for table_ref, cosine, sine in (
        (left_table_ref, tables_ref[2], -tables_ref[3]),
        (right_table_ref, tables_ref[4], tables_ref[5]),
    ):
        table_ref[low, low] = cosine
        table_ref[high, high] = cosine
        table_ref[low, high] = sine
        table_ref[high, low] = -sine
    fetches[6].wait()

    def go_forward(mode, carry):
        fetch_probe(mode).wait()
        probe_real, probe_imag = probe_ref[0, mode], probe_ref[1, mode]
        waves = []
        for slot in range(slots):
            win_real, win_imag = window_ref[slot, 0], window_ref[slot, 1]
            waves.append(
                (
                    probe_real * win_real - probe_imag * win_imag,
                    probe_real * win_imag + probe_imag * win_real,
                )
            )
        far = folded_pass(waves, tables_ref[0], tables_ref[1])
        far_ref[mode] = far
        far_real, far_imag = far[:, :length], far[:, length:]
        level_ref[...] += far_real * far_real + far_imag * far_imag
        return carry

    lax.fori_loop(0, modes, go_forward, 0, unroll=UNROLL)
    amplitude = jnp.maximum(jnp.sqrt(level_ref[...]), 1.0)
    targets = jnp.concatenate([pattern_ref[slot] for slot in range(slots)], axis=0)
    level_ref[...] = 1.0 - targets / amplitude

    def go_back(mode, carry):
        corrected = []
        for slot in range(slots):
            band = slice(slot * length, (slot + 1) * length)
            factor = level_ref[band]
            far = far_ref[mode, band]
            corrected.append((factor * far[:, :length], factor * far[:, length:]))
        back = fourier_pass(stacked(corrected), left_table_ref[...], right_table_ref[...])
        probe_real, probe_imag = probe_ref[0, mode], probe_ref[1, mode]
        term_real = term_imag = 0.0
        for slot in range(slots):
            band = slice(slot * length, (slot + 1) * length)
            back_real, back_imag = back[band, :length], back[band, length:]
            object_ref[slot, 0] += probe_real * back_real + probe_imag * back_imag
            object_ref[slot, 1] += probe_real * back_imag - probe_imag * back_real
            win_real, win_imag = window_ref[slot, 0], window_ref[slot, 1]
            term_real += win_real * back_real + win_imag * back_imag
            term_imag += win_real * back_imag - win_imag * back_real
        mine_ref[mode] = jnp.where(first, term_real, term_imag)
        other_ref[mode] = jnp.where(first, term_imag, term_real)
        return carry

    lax.fori_loop(0, modes, go_back, 0, unroll=UNROLL)
    for slot in range(slots):
        span, shift, col = places[slot]
        for part in range(2):
            strip = jnp.concatenate(
                [object_ref[slot, part], jnp.zeros((8, length), jnp.float32)], axis=0
            )
            strip = pltpu.roll(strip, shift, 0)
            strip = jnp.concatenate(
                [strip, jnp.zeros((length + 8, wide - length), jnp.float32)], axis=1
            )
            strip = pltpu.roll(strip, col, 1)
            rim_left_ref[part, span, :] += strip[:, :half]
            center_ref[part, span, :] += strip[:, half : half + cols]
            rim_right_ref[part, span, :] += strip[:, half + cols :]


def device_gradients(place, block, above, below, left, right, probe, pattern):
    tables = fourier_tables(probe.shape[-1])
    _, modes, length, _ = probe.shape
    rows, cols = block.shape[1] + length, block.shape[2] + length
    slots = pattern.shape[0]
    anywhere = pl.BlockSpec(memory_space=pl.ANY)
    f32 = jnp.float32
    fetched = (block, above, below, left, right, probe, pattern, tables)
    made = (
        jax.ShapeDtypeStruct((2, rows, length // 2), f32),
        jax.ShapeDtypeStruct((2, rows, block.shape[2]), f32),
        jax.ShapeDtypeStruct((2, rows, length // 2), f32),
        jax.ShapeDtypeStruct((modes, length, length), f32),
        jax.ShapeDtypeStruct((modes, length, length), f32),
    )
    return pl.pallas_call(
        gradients_kernel,
        out_shape=made,
        in_specs=[pl.BlockSpec(memory_space=pltpu.SMEM)] + [anywhere] * len(fetched),
        out_specs=(pl.BlockSpec(memory_space=pltpu.VMEM),) * len(made),
        scratch_shapes=[pltpu.VMEM(item.shape, item.dtype) for item in fetched]
        + [
            pltpu.VMEM((2 * length, 2 * length), jnp.bfloat16),
            pltpu.VMEM((2 * length, 2 * length), jnp.bfloat16),
            pltpu.VMEM((2, rows, cols), f32),
            pltpu.VMEM((slots, 2, length, length), f32),
            pltpu.VMEM((modes, slots * length, 2 * length), f32),
            pltpu.VMEM((slots * length, length), f32),
            pltpu.VMEM((slots, 2, length, length), f32),
            pltpu.SemaphoreType.DMA((modes,)),
            pltpu.SemaphoreType.DMA((8,)),
        ],
        compiler_params=pltpu.CompilerParams(vmem_limit_bytes=GRANT * 1024 * 1024),
        cost_estimate=pl.CostEstimate(
            flops=slots * modes * 32 * length**3, bytes_accessed=16 * 2**20, transcendentals=0
        ),
    )(place, *fetched)


def axis_groups(kept):
    rows, cols = lax.axis_size("region"), lax.axis_size("scan")
    sizes = {"core": 2, "x": cols // 2, "y": 4, "pair": 2, "far": rows // 8}
    groups = {}
    for device in range(rows * cols):
        place, rest = {}, device
        for name in sizes:
            place[name] = rest % sizes[name]
            rest = rest // sizes[name]
        key = tuple(place[name] for name in place if name not in kept)
        groups.setdefault(key, []).append(device)
    return [groups[key] for key in sorted(groups)]


def narrow(values, scale):
    return (values * (1.0 / scale)).astype(jnp.float16)


def widen(values, scale):
    return values.astype(jnp.float32) * scale


def exchange(parts, kept):
    return lax.all_to_all(parts, ("region", "scan"), 0, 0, axis_index_groups=axis_groups(kept))


def swap_cores(values):
    count = lax.axis_size("region") * lax.axis_size("scan")
    return lax.ppermute(values, ("region", "scan"), [(i, i ^ 1) for i in range(count)])


def shift_far(values, step):
    cols = lax.axis_size("scan")
    count = lax.axis_size("region") * cols
    stride = 8 * cols
    pairs = [(i, (i + step * stride) % count) for i in range(count)]
    return lax.ppermute(values, ("region", "scan"), pairs)


def sum_scattered(mine, other):
    modes, rows, cols = mine.shape
    pair = mine + widen(swap_cores(narrow(other, 8.0)), 8.0)
    places = 8 * (lax.axis_size("scan") // 2)
    pieces = narrow(pair, 16.0).reshape(places, modes * rows // places, cols)
    pieces = exchange(pieces, ("pair", "y", "x"))
    return jnp.sum(widen(pieces, 16.0), axis=0)


def sum_far(piece):
    sent = narrow(piece, 512.0)
    one, two, three = (widen(shift_far(sent, step), 512.0) for step in (1, 2, 3))
    return (widen(sent, 512.0) + two) + (one + three)


def gather_all(total, modes):
    rows, cols = total.shape
    places = 8 * (lax.axis_size("scan") // 2)
    pieces = jnp.broadcast_to(total, (places, rows, cols))
    return exchange(pieces, ("pair", "y", "x")).reshape(modes, -1, cols)


def neighbours(head, tail, axis, kind):
    count = lax.axis_size(axis)
    even = lax.axis_index(axis) % 2 == 0
    swaps = [
        [pair for i in range(start, count - 1, 2) for pair in ((i, i + 1), (i + 1, i))]
        for start in (0, 1)
    ]
    outer = lax.ppermute(jnp.where(even, head, tail).astype(kind), axis, swaps[1])
    inner = lax.ppermute(jnp.where(even, tail, head).astype(kind), axis, swaps[0])
    return (jnp.where(even, outer, inner), jnp.where(even, inner, outer))


def trade(head, tail, axis):
    return neighbours(narrow(head, 64.0), narrow(tail, 64.0), axis, jnp.float16)


def on_device(object_field, probe_modes, pattern, rows_at, cols_at, object_step, probe_step):
    half_width = probe_modes.shape[-1] // 2
    block_rows = object_field.shape[1]
    block_cols = object_field.shape[2]
    core = lax.axis_index("scan") % 2
    place = jnp.stack(
        [
            rows_at[0, 0] % block_rows,
            cols_at[0, 0] % block_cols,
            jnp.broadcast_to(core, rows_at.shape[2:]).astype(jnp.int32),
        ]
    )
    targets = jnp.sqrt(pattern[0, 0])
    for dim in (1, 2):
        nearer = lax.slice_in_dim(targets, 0, half_width + 1, axis=dim)
        farther = lax.slice_in_dim(targets, half_width + 1, 2 * half_width, axis=dim)
        targets = jnp.concatenate([nearer, lax.rev(farther, (dim,))], axis=dim)
    kind = jnp.bfloat16
    above, below = neighbours(
        object_field[:, :half_width], object_field[:, -half_width:], "region", kind
    )
    sides = [
        jnp.concatenate([above[:, :, cut], object_field[:, :, cut].astype(kind), below[:, :, cut]], 1)
        for cut in (slice(0, half_width), slice(block_cols - half_width, block_cols))
    ]
    left, right = neighbours(*sides, "scan", kind)
    rim_left, center, rim_right, mine, other = device_gradients(
        place, object_field, above, below, left, right, probe_modes, targets
    )
    piece = sum_scattered(mine, other)
    from_left, from_right = trade(rim_left, rim_right, "scan")
    center = center + widen(jnp.concatenate([from_left, from_right], axis=2), 64.0)
    region, scan = lax.axis_index("region"), lax.axis_index("scan")
    spot = (region % 8 * 4 + scan // 2) * piece.shape[0]
    flat = probe_modes.reshape(2, -1, probe_modes.shape[-1])
    mine = lax.dynamic_slice(flat, (core, spot, 0), (1, *piece.shape))[0]
    piece, mine = lax.optimization_barrier((piece, mine))
    total = sum_far(piece)
    updated = narrow(mine - probe_step[0] * total, 128.0)
    updated, center = lax.optimization_barrier((updated, center))
    from_above, from_below = trade(center[:, :half_width], center[:, -half_width:], "region")
    plane = gather_all(updated, probe_modes.shape[1])
    plane, from_above, from_below = lax.optimization_barrier((plane, from_above, from_below))
    swapped = swap_cores(plane)
    inner = center[:, half_width:-half_width]
    inner = inner + widen(jnp.concatenate([from_above, from_below], axis=1), 64.0)
    object_field = object_field - object_step[0] * inner
    own = lax.broadcasted_iota(jnp.int32, probe_modes.shape, 0) == core
    probe_modes = widen(jnp.where(own, plane[None], swapped[None]), 128.0)
    return (object_field, probe_modes)


def solution(mesh):
    return jax.shard_map(
        on_device,
        mesh=mesh,
        in_specs=(
            P(None, "region", "scan"),
            P(),
            P("region", "scan", None, None, None),
            P("region", "scan", None),
            P("region", "scan", None),
            P(),
            P(),
        ),
        out_specs=(P(None, "region", "scan"), P()),
        check_vma=False,
    )
```
